128 devices in a mesh: blk: 8 (over y, z_hi), expert: 16 (over z_lo, x, core).
Axes of the slice: x: 4, y: 4, z: 4 (z_hi: 2, z_lo: 2; z = z_hi * 2 + z_lo), core: 2. Of those that a mesh axis runs over, the one named last changes fastest.
Arguments:
- query: bfloat16 [16, 1024, 4096], P('expert', 'blk'), may hold values from -16 to 16
- keys: bfloat16 [16, 1024, 256], P('expert', 'blk'), may hold values from -16 to 16
- values: bfloat16 [16, 1024, 256], P('expert', 'blk'), may hold values from -6 to 6
- grad_output: bfloat16 [16, 1024, 4096], P('expert', 'blk'), may hold values from -6 to 6
- expert_ids: int32 [16, 1024, 8], P('expert', 'blk'), may hold values from 0 to 127, all different within a row; in each aligned block of 128 rows (0 to 127, 128 to 255, ..., all dimensions but the last counted through in order) at most 9 rows name the same one
- gate_weights: float32 [16, 1024, 8], P('expert', 'blk'), may hold values from 0.05 to 0.5
- gate_up: bfloat16 [128, 4096, 1536], P(('blk', 'expert')), may hold values from -0.09375 to 0.09375
- down_weight: bfloat16 [128, 768, 4096], P(('blk', 'expert')), may hold values from -0.21875 to 0.21875
- saved_preact: bfloat16 [128, 128, 9, 1536], P(('blk', 'expert')), may hold values from -6 to 6
- block_order: int32 [16], replicated, may hold values from 0 to 15, each once
Outputs:
- query_gradient: bfloat16 [16, 1024, 4096], P('expert', 'blk')
- key_gradient: bfloat16 [16, 1024, 256], P('expert', 'blk')
- value_gradient: bfloat16 [16, 1024, 256], P('expert', 'blk')
The draws below stay inside these ranges and needn't reach their ends.
Inputs may be any that keep to these rules, and one draw needn't show every extreme that they name: `expert_ids`: each token names 8 different experts; the 128 tokens of one device name one expert at most 9 times, and some device's tokens name some expert exactly 9 times.
All inputs are finite; a program needn't handle non-finite values.
Results may differ from the reference program's by a relative error of at most 0.019.
Values may be sent and summed in bfloat16 or wider, within the bound.
A program may use at most 192 MiB of HBM per device.

```python
import math
import jax
import jax.numpy as jnp
import numpy as np
from jax import lax

D = 4096
QUERY_HEADS = 32
KEY_VALUE_HEADS = 2
HEAD_SIZE = 128
FF = 768
TOP = 8
TOK_DEV = 128
EXPERTS = 128
SEQUENCE_COUNT = 16
SEQUENCE_TOKENS = 1024
CH = 64
MOST = 9
N_BLK = 8
DEVICES = 128


def draw_query(key, part):
    key = jax.random.fold_in(key, 11)
    base_offset = 1.5 * jnp.clip(jax.random.normal(key, (SEQUENCE_COUNT, SEQUENCE_TOKENS, QUERY_HEADS * HEAD_SIZE), jnp.float32), -3.0, 3.0)
    return base_offset.astype(jnp.bfloat16)


def draw_keys(key, part):
    key = jax.random.fold_in(key, 23)
    base_offset = jnp.clip(jax.random.normal(key, (SEQUENCE_COUNT, SEQUENCE_TOKENS, KEY_VALUE_HEADS * HEAD_SIZE), jnp.float32), -4.0, 4.0)
    return base_offset.astype(jnp.bfloat16)


def level_of(rng, dims, split, low, high):
    def one(axis_at, blocks):
        steps = jax.random.uniform(jax.random.fold_in(jax.random.fold_in(rng, 6), axis_at), (blocks,), jnp.float32, low / len(split), high / len(split))
        return jnp.repeat(jnp.exp(steps), dims[axis_at] // blocks).reshape((-1,) + (1,) * (len(dims) - axis_at - 1))

    factor_of = one(*split[0])
    for cut in split[1:]:
        factor_of = factor_of * one(*cut)
    return factor_of


def shared_out(rng, own, number, rows, amount, top, most, lean):
    sequence = jax.random.permutation(rng, amount)
    packed, ordinary = shares(amount, rows * top, most, lean, True), shares(amount, rows * top, most, lean, False)
    places = jnp.arange(amount)

    def named(sizes, offset_by):
        used = int((sizes > 0).sum())
        fixed = max(1, used // 4)
        moved = fixed + (places - fixed + offset_by * (used - fixed)) % max(1, amount - fixed)
        return jnp.zeros((amount,), jnp.int32).at[sequence[jnp.where(places < fixed, places, moved)]].set(jnp.asarray(sizes, jnp.int32))

    sizes = jnp.where(number % 4 == 0, named(packed, number // 4), named(ordinary, number - number // 4 - 1))
    mixed = jax.random.permutation(jax.random.fold_in(own, 3), amount)
    source_of, receiver = mixed[0:amount // 2 * 2:2], mixed[1:amount // 2 * 2:2]
    slack = jnp.minimum(sizes[source_of] - 1, most - sizes[receiver]) // 2
    slack = jnp.where((source_of == sequence[0]) | (receiver == sequence[0]) | (sizes[receiver] == 0), 0, jnp.maximum(slack, 0))
    moved = jax.random.randint(jax.random.fold_in(own, 4), (amount // 2,), 0, 1 << 20) % (slack + 1)
    sizes = sizes.at[source_of].add(-moved).at[receiver].add(moved)
    labels = jnp.searchsorted(jnp.cumsum(sizes), jnp.arange(rows * top), side="right").astype(jnp.int32)
    table = labels.reshape(top, rows).T
    table = table[jax.random.permutation(jax.random.fold_in(own, 1), rows)]
    offset_by = jax.random.randint(jax.random.fold_in(own, 2), (rows, 1), 0, top)
    return jnp.take_along_axis(table, (jnp.arange(top)[None, :] + offset_by) % top, axis=1)


def shares(count, total, bound, lean, full):
    weights = [(1 << 20) // math.isqrt(standing ** lean) + 1 for standing in range(1, count + 1)]
    largest = bound if full else min(bound, max(-(-total // count), total * weights[0] // sum(weights)))
    least = 1 if total - largest >= count - 1 else 0
    given, surplus = [largest] + [least] * (count - 1), total - largest - least * (count - 1)
    while surplus > 0:
        movable = [i for i in range(1, count) if given[i] < largest] or [i for i in range(1, count) if given[i] < bound]
        whole, left = sum([weights[i] for i in movable]), surplus
        for i in movable:
            extra = min(bound - given[i], max(1, left * weights[i] // whole), surplus)
            given[i] = given[i] + extra
            surplus = surplus - extra
    return np.array(given)


def scatter_about(key, extent, scale, reach, shards=(), kind=jnp.bfloat16):
    drawn = scale * jax.random.normal(key, extent, jnp.float32)
    if shards:
        drawn = drawn * level_of(key, extent, shards, -0.22, 0.18)
    return jnp.clip(drawn, -reach, reach).astype(kind)


def setup_inputs(seed: int = 0) -> dict:
    arg_keys = jax.random.split(jax.random.key(seed), 11)
    query = draw_query(jax.random.fold_in(arg_keys[10], 71), 0)
    keys = draw_keys(jax.random.fold_in(arg_keys[10], 71), 0)
    values = scatter_about(arg_keys[2], (SEQUENCE_COUNT, SEQUENCE_TOKENS, KEY_VALUE_HEADS * HEAD_SIZE), 1.0, 6.0, ((0, 16), (1, 8)))
    grad_output = scatter_about(arg_keys[3], (SEQUENCE_COUNT, SEQUENCE_TOKENS, D), 1.0, 6.0, ((0, 16), (1, 8)))
    expert_ids_keys = jax.random.split(jax.random.fold_in(arg_keys[4], 1), SEQUENCE_COUNT * SEQUENCE_TOKENS // TOK_DEV)
    expert_ids_turns = jax.random.permutation(jax.random.fold_in(arg_keys[4], 3), SEQUENCE_COUNT * SEQUENCE_TOKENS // TOK_DEV)
    expert_ids = jax.vmap(lambda own, number: shared_out(jax.random.fold_in(arg_keys[4], 2), own, number, TOK_DEV, EXPERTS, TOP, MOST, 2))(expert_ids_keys, expert_ids_turns).reshape((SEQUENCE_COUNT, SEQUENCE_TOKENS, TOP))
    gate_weights = jnp.clip(jnp.exp(math.log(0.5) - 2.3025851 * jax.random.uniform(arg_keys[5], (SEQUENCE_COUNT, SEQUENCE_TOKENS, TOP), jnp.float32) ** level_of(arg_keys[5], (SEQUENCE_COUNT, SEQUENCE_TOKENS, TOP), ((0, 16), (1, 8)), -0.2, 0.2)), 0.05, 0.5)
    gate_up = scatter_about(arg_keys[6], (EXPERTS, D, 2 * FF), D ** -0.5, 0.09375, ((0, 128),))
    down_weight = scatter_about(arg_keys[7], (EXPERTS, FF, D), FF ** -0.5, 0.21875, ((0, 128),))
    saved_preact = scatter_about(arg_keys[8], (EXPERTS, DEVICES, MOST, 2 * FF), 1.5, 6.0, ((0, 128),))
    block_order = jax.random.permutation(arg_keys[9], 2 * N_BLK).astype(jnp.int32)
    return {"query": query, "keys": keys, "values": values, "grad_output": grad_output, "expert_ids": expert_ids, "gate_weights": gate_weights, "gate_up": gate_up, "down_weight": down_weight, "saved_preact": saved_preact, "block_order": block_order}


def rounded(array):
    return lax.optimization_barrier(array.astype(jnp.bfloat16)).astype(jnp.float32)

def slot_numbers(flat_ids):
    onehot = (flat_ids[:, None] == jnp.arange(EXPERTS, dtype=jnp.int32)[None, :]).astype(jnp.int32)
    before = jnp.cumsum(onehot, axis=0) - onehot
    return lax.optimization_barrier(jnp.sum(before * onehot, axis=1)).astype(jnp.int32)

def swiglu_grad(down_grad, saved):
    width = saved.shape[1] // 2
    gate = saved[:, :width]
    upper = saved[:, width:]
    sigma = jax.nn.sigmoid(gate)
    gate_grad = down_grad * upper * sigma * (1.0 + gate * (1.0 - sigma))
    upper_grad = down_grad * gate * sigma
    return jnp.concatenate([gate_grad, upper_grad], axis=1)

def by_device(array):
    rest = array.shape[2:]
    shaped = array.reshape((SEQUENCE_COUNT, N_BLK, TOK_DEV) + rest)
    return jnp.swapaxes(shaped, 0, 1).reshape((N_BLK * SEQUENCE_COUNT, TOK_DEV) + rest)

def reference(query, keys, values, grad_output, expert_ids, gate_weights, gate_up, down_weight, saved_preact, block_order):
    device_count = N_BLK * SEQUENCE_COUNT
    dev_grad = by_device(grad_output)
    dev_ids = by_device(expert_ids).reshape(device_count, TOK_DEV * TOP)
    dev_gates = by_device(gate_weights).reshape(device_count, TOK_DEV * TOP)
    dev_slots = jax.vmap(slot_numbers)(dev_ids)
    token_of = jnp.arange(TOK_DEV * TOP, dtype=jnp.int32) // TOP
    source = jnp.broadcast_to(jnp.arange(device_count, dtype=jnp.int32)[:, None], dev_ids.shape)
    table = jnp.full((EXPERTS, device_count, MOST), TOK_DEV, jnp.int32)
    table = table.at[dev_ids, source, dev_slots].set(jnp.broadcast_to(token_of[None, :], dev_ids.shape))
    padded = jnp.concatenate([dev_grad, jnp.zeros((device_count, 1, D), dev_grad.dtype)], axis=1)
    sources = jnp.arange(device_count, dtype=jnp.int32)[:, None]

    def expert_pass(index):
        rows = padded[sources, table[index]].reshape(device_count * MOST, D)
        down_grad = jnp.dot(rows, down_weight[index].T, preferred_element_type=jnp.float32)
        saved = saved_preact[index].reshape(device_count * MOST, 2 * FF).astype(jnp.float32)
        act_grad = swiglu_grad(down_grad, saved).astype(jnp.bfloat16)
        back = jnp.dot(act_grad, gate_up[index].T, preferred_element_type=jnp.float32).astype(jnp.bfloat16)
        return back.reshape(device_count, MOST, D)
    returned = lax.map(expert_pass, jnp.arange(EXPERTS, dtype=jnp.int32))

    def combine(device):
        picked = returned[dev_ids[device], device, dev_slots[device]].astype(jnp.float32)
        weighted = lax.optimization_barrier(jnp.sum((picked * dev_gates[device][:, None]).reshape(TOK_DEV, TOP, D), axis=1))
        return (dev_grad[device].astype(jnp.float32) + weighted).astype(jnp.bfloat16)
    dev_residual = lax.map(combine, jnp.arange(device_count, dtype=jnp.int32))
    residual_grad = jnp.swapaxes(dev_residual.reshape(N_BLK, SEQUENCE_COUNT, TOK_DEV, D), 0, 1).reshape(SEQUENCE_COUNT, SEQUENCE_TOKENS, D)
    rows_all = jnp.arange(SEQUENCE_TOKENS, dtype=jnp.int32)
    position = block_order[rows_all // CH] * CH + rows_all % CH
    visible = position[:, None] >= position[None, :]
    group_width = QUERY_HEADS // KEY_VALUE_HEADS
    scale = HEAD_SIZE ** (-0.5)

    def one_sequence(items):
        query_sequence, key_sequence, value_sequence, gradient_sequence = items
        query_four = query_sequence.reshape(SEQUENCE_TOKENS, KEY_VALUE_HEADS, group_width, HEAD_SIZE).astype(jnp.float32)
        keys_three = key_sequence.reshape(SEQUENCE_TOKENS, KEY_VALUE_HEADS, HEAD_SIZE).astype(jnp.float32)
        values_three = value_sequence.reshape(SEQUENCE_TOKENS, KEY_VALUE_HEADS, HEAD_SIZE).astype(jnp.float32)
        gradient_four = gradient_sequence.reshape(SEQUENCE_TOKENS, KEY_VALUE_HEADS, group_width, HEAD_SIZE).astype(jnp.float32)
        scores = jnp.einsum('pgjd,rgd->gjpr', query_four, keys_three) * scale
        row_max = lax.optimization_barrier(jnp.max(jnp.where(visible, scores, -1e+30), axis=-1))
        fwd_weights = jnp.where(visible, jnp.exp(scores - row_max[..., None]), 0.0)
        total = lax.optimization_barrier(jnp.sum(fwd_weights, axis=-1))
        attn_out = jnp.einsum('gjpr,rgd->gjpd', rounded(fwd_weights), values_three) / total[..., None]
        log_total = row_max + jnp.log(total)
        delta = lax.optimization_barrier(jnp.sum(jnp.transpose(gradient_four, (1, 2, 0, 3)) * attn_out, axis=-1))
        probs = jnp.where(visible, jnp.exp(scores - log_total[..., None]), 0.0)
        value_gradient = jnp.einsum('gjpr,pgjd->rgd', rounded(probs), gradient_four)
        prob_grad = jnp.einsum('pgjd,rgd->gjpr', gradient_four, values_three)
        score_grad = rounded(probs * (prob_grad - delta[..., None]))
        query_gradient = jnp.einsum('gjpr,rgd->pgjd', score_grad, keys_three) * scale
        key_gradient = jnp.einsum('gjpr,pgjd->rgd', score_grad, query_four) * scale
        return (query_gradient.reshape(SEQUENCE_TOKENS, QUERY_HEADS * HEAD_SIZE).astype(jnp.bfloat16), key_gradient.reshape(SEQUENCE_TOKENS, KEY_VALUE_HEADS * HEAD_SIZE).astype(jnp.bfloat16), value_gradient.reshape(SEQUENCE_TOKENS, KEY_VALUE_HEADS * HEAD_SIZE).astype(jnp.bfloat16))
    query_gradient, key_gradient, value_gradient = lax.map(one_sequence, (query, keys, values, residual_grad))
    return (query_gradient, key_gradient, value_gradient)
```

```python
import math

import jax
import jax.numpy as jnp
from jax import lax
from jax.experimental import pallas as pl
from jax.experimental.pallas import tpu as pltpu
from jax.sharding import PartitionSpec as P

MESH = pl.DeviceIdType.MESH
HEAD = 128
ORDERS = ((0, 1, 2), (1, 2, 0), (2, 0, 1))
BF = jnp.bfloat16
F32 = jnp.float32


def coords():
    b = lax.axis_index("blk")
    e = lax.axis_index("expert")
    return (e // 2) % 4, b // 2, (b % 2) * 2 + e // 8, e % 2


def device_of(x, y, z, c):
    return (y * 2 + z // 2, ((z % 2) * 4 + x) * 2 + c)


def exchange_kernel(
    tok, ret, wts,
    g_ref, k_ref, v_ref, saved_ref, down_ref, gate_ref,
    res_ref, kf_ref, vf_ref,
    S, A, B, R, X, act, D, G, sv,
    ssem, rsem, lsem, kvs, kvr, dsem, gsem, svsem,
):
    x, y, z, c = coords()
    cc = (x, y, z)
    bme = lax.axis_index("blk")
    eme = lax.axis_index("expert")

    def dv(dim, v, core):
        t = [x, y, z]
        t[dim] = v
        return device_of(t[0], t[1], t[2], core)

    barrier = pltpu.get_barrier_semaphore()
    peers = [dv(dim, (cc[dim] + k) & 3, c ^ dc) for dim in range(3) for k in range(1, 4) for dc in range(2)]
    peers.append(dv(0, x, c ^ 1))
    peers += [device_of(x, (y + k) & 3, z ^ 2, c) for k in range(1, 4)]
    for p in peers:
        pl.semaphore_signal(barrier, inc=1, device_id=p, device_id_type=MESH)

    pltpu.make_async_copy(down_ref, D, dsem).start()

    def gate_copy(block, slot):
        return pltpu.make_async_copy(gate_ref.at[pl.ds(block * 512, 512)], G.at[slot], gsem.at[slot])

    def saved_copy(j):
        return pltpu.make_async_copy(saved_ref.at[pl.ds(3 * j, 3)], sv, svsem)

    gate_copy(0, 0).start()
    gate_copy(1, 1).start()
    saved_copy(0).start()

    def build(j):
        def body(i, carry):
            for u in range(8):
                row = j * 384 + i * 8 + u
                S[j * 12 + i // 4, i % 4, u] = g_ref[tok[row]]
            return carry

        lax.fori_loop(0, 48, body, 0)

    build(0)
    pl.semaphore_wait(barrier, len(peers))

    def remote(src, dst, ph, j, q, dev):
        return pltpu.make_async_remote_copy(
            src, dst, ssem.at[ph, j, q], rsem.at[ph, j, q], device_id=dev, device_id_type=MESH
        )

    def phase(ph, j):
        for k in (2, 1, 3, 0):
            for q, (a, b, d) in enumerate(ORDERS):
                ma, mb, md = cc[a], cc[b], cc[d]
                n = 3 * j + q
                if ph in (0, 5):
                    v = (ma + k) & 3
                    if ph == 0:
                        ops = [(S.at[n * 4 + v], A.at[n, ma], dv(a, v, c), k == 0)]
                    else:
                        ops = [(A.at[n, v], S.at[n * 4 + ma], dv(a, v, c), k == 0)]
                elif ph in (1, 4):
                    v = (mb + k) & 3
                    if ph == 1:
                        ops = [(A.at[n, :, v], B.at[n, pl.ds(mb * 4, 4)], dv(b, v, c), k == 0)]
                    else:
                        ops = [(B.at[n, pl.ds(v * 4, 4)], A.at[n, :, mb], dv(b, v, c), k == 0)]
                else:
                    v = (md + k) & 3
                    ops = []
                    for dc in range(2):
                        t = c ^ dc
                        here = k == 0 and dc == 0
                        if ph == 2:
                            ops.append(
                                (B.at[n, :, v * 2 + t], R.at[n, pl.ds((md * 2 + c) * 16, 16)], dv(d, v, t), here)
                            )
                        else:
                            ops.append(
                                (R.at[n, pl.ds((v * 2 + t) * 16, 16)], B.at[n, :, md * 2 + c], dv(d, v, t), here)
                            )
                for src, dst, dev, here in ops:
                    if here:
                        pltpu.make_async_copy(src, dst, lsem.at[ph, j, q]).start()
                    else:
                        remote(src, dst, ph, j, q, dev).start()

    def wait(ph, j):
        for q in range(3):
            if ph in (2, 3):
                far = R.at[0, pl.ds(0, 112)]
                near = R.at[0, pl.ds(0, 16)]
            else:
                far = R.at[0, pl.ds(0, 96)]
                near = R.at[0, pl.ds(0, 32)]
            pltpu.make_async_copy(far, far, rsem.at[ph, j, q]).wait()
            pltpu.make_async_copy(near, near, lsem.at[ph, j, q]).wait()
            pltpu.make_async_copy(far, far, ssem.at[ph, j, q]).wait()

    rows = lax.broadcasted_iota(jnp.int32, (256, 256), 0)
    cols = lax.broadcasted_iota(jnp.int32, (256, 256), 1)
    perm = jnp.where(cols == (rows & 15) * 16 + (rows >> 4), 1.0, 0.0).astype(BF)

    def experts(j):
        def unpack(i, carry):
            n = 3 * j + i // 8
            r0 = pl.multiple_of((i % 8) * 16, 16)
            x0 = pl.multiple_of(i * 16, 16)
            lo = R[n, pl.ds(r0, 16), :16, :].reshape(256, 128)
            hi = R[n, pl.ds(r0, 16), 16:, :].reshape(256, 128)
            out = jnp.dot(perm, jnp.concatenate([lo, hi], axis=1), preferred_element_type=F32).astype(BF)
            for u in range(16):
                X[pl.ds(x0, 16), u * 128 : (u + 1) * 128] = out[u * 16 : (u + 1) * 16, :128]
                X[pl.ds(x0, 16), 2048 + u * 128 : 2048 + (u + 1) * 128] = out[u * 16 : (u + 1) * 16, 128:]
            return carry

        lax.fori_loop(0, 24, unpack, 0)
        if j == 0:
            pltpu.make_async_copy(down_ref, D, dsem).wait()
        saved_copy(j).wait()

        def first(i, carry):
            at = pl.multiple_of(i * 256, 256)
            dg = lax.dot_general(
                X[...], D[pl.ds(at, 256), :], (((1,), (1,)), ((), ())), preferred_element_type=F32
            )
            gate = sv[:, :, pl.ds(at, 256)].reshape(384, 256).astype(F32)
            upper = sv[:, :, pl.ds(768 + at, 256)].reshape(384, 256).astype(F32)
            sigma = 1.0 / (1.0 + jnp.exp(-gate))
            ds = dg * sigma
            act[:, pl.ds(at, 256)] = (ds * upper * (1.0 + gate * (1.0 - sigma))).astype(BF)
            act[:, pl.ds(768 + at, 256)] = (ds * gate).astype(BF)
            return carry

        lax.fori_loop(0, 3, first, 0)
        if j < 2:
            saved_copy(j + 1).start()

        def second(i, carry):
            slot = i % 2
            gate_copy(i, slot).wait()
            at = pl.multiple_of(i * 512, 512)
            X[:, pl.ds(at, 512)] = lax.dot_general(
                act[...], G[slot], (((1,), (1,)), ((), ())), preferred_element_type=F32
            ).astype(BF)
            if j < 2:
                gate_copy((i + 2) % 8, slot).start()
            else:
                @pl.when(i < 6)
                def _():
                    gate_copy(i + 2, slot).start()
            return carry

        lax.fori_loop(0, 8, second, 0)

        def pack(i, carry):
            n = 3 * j + i // 8
            r0 = pl.multiple_of((i % 8) * 16, 16)
            x0 = pl.multiple_of(i * 16, 16)
            lo = jnp.concatenate([X[pl.ds(x0, 16), u * 128 : (u + 1) * 128] for u in range(16)], axis=0)
            hi = jnp.concatenate([X[pl.ds(x0, 16), 2048 + u * 128 : 2048 + (u + 1) * 128] for u in range(16)], axis=0)
            out = jnp.dot(perm, jnp.concatenate([lo, hi], axis=1), preferred_element_type=F32).astype(BF)
            R[n, pl.ds(r0, 16), :16, :] = out[:, :128].reshape(16, 16, 128)
            R[n, pl.ds(r0, 16), 16:, :] = out[:, 128:].reshape(16, 16, 128)
            return carry

        lax.fori_loop(0, 24, pack, 0)

    def kv_copies():
        for k in range(1, 8):
            to = (bme + k) & 7
            for src, dst, t in ((k_ref, kf_ref, 0), (v_ref, vf_ref, 1)):
                yield pltpu.make_async_remote_copy(
                    src, dst.at[bme], kvs.at[t], kvr.at[t], device_id=(to, eme), device_id_type=MESH
                )

    for step in range(9):
        active = [(ph, step - ph - (1 if ph >= 3 else 0)) for ph in range(6)]
        active = [(ph, j) for ph, j in active if 0 <= j < 3]
        for ph, j in active:
            phase(ph, j)
        if step == 0:
            kf_ref[bme] = k_ref[...]
            vf_ref[bme] = v_ref[...]
            for copy in kv_copies():
                copy.start()
            build(1)
            build(2)
        if 3 <= step < 6:
            experts(step - 3)
        for ph, j in active:
            wait(ph, j)

    for t, full in ((0, kf_ref), (1, vf_ref)):
        seven = full.at[pl.ds(0, 7)]
        pltpu.make_async_copy(seven, seven, kvr.at[t]).wait()
        pltpu.make_async_copy(seven, seven, kvs.at[t]).wait()

    def combine(t, carry):
        total = g_ref[t].astype(F32)
        for k in range(8):
            at = ret[t * 8 + k]
            total += wts[t * 8 + k] * S[at // 32, (at // 8) % 4, at % 8].astype(F32)
        res_ref[t] = total.astype(BF)
        return carry

    lax.fori_loop(0, 128, combine, 0)


def exchange(tok, ret, wts, g3, keys, values, saved, down, gate):
    smem = pl.BlockSpec(memory_space=pltpu.SMEM)
    vmem = pl.BlockSpec(memory_space=pltpu.VMEM)
    hbm = pl.BlockSpec(memory_space=pl.ANY)
    row = (32, 128)
    return pl.pallas_call(
        exchange_kernel,
        out_shape=(
            jax.ShapeDtypeStruct((128,) + row, BF),
            jax.ShapeDtypeStruct((8, 128, 256), BF),
            jax.ShapeDtypeStruct((8, 128, 256), BF),
        ),
        in_specs=[smem, smem, smem, vmem, vmem, vmem, hbm, hbm, hbm],
        out_specs=(vmem, vmem, vmem),
        scratch_shapes=[
            pltpu.VMEM((36, 4, 8) + row, BF),
            pltpu.VMEM((9, 4, 4, 8) + row, BF),
            pltpu.VMEM((9, 16, 8) + row, BF),
            pltpu.VMEM((9, 128) + row, BF),
            pltpu.VMEM((384, 4096), BF),
            pltpu.VMEM((384, 1536), BF),
            pltpu.VMEM((768, 4096), BF),
            pltpu.VMEM((2, 512, 1536), BF),
            pltpu.VMEM((3, 128, 1536), BF),
            pltpu.SemaphoreType.DMA((6, 3, 3)),
            pltpu.SemaphoreType.DMA((6, 3, 3)),
            pltpu.SemaphoreType.DMA((6, 3, 3)),
            pltpu.SemaphoreType.DMA((2,)),
            pltpu.SemaphoreType.DMA((2,)),
            pltpu.SemaphoreType.DMA,
            pltpu.SemaphoreType.DMA((2,)),
            pltpu.SemaphoreType.DMA,
        ],
        compiler_params=pltpu.CompilerParams(
            collective_id=0, has_side_effects=True, vmem_limit_bytes=63 << 20
        ),
    )(tok, ret, wts, g3, keys, values, saved, down, gate)


def attention_kernel(
    q_ref, res_ref, k_ref, v_ref, posq_ref, posk_ref,
    dq_ref, dk_out, dv_out,
    kt, vt, dk_acc, dv_acc, part, got, ssem, rsem,
):
    bme = lax.axis_index("blk")
    eme = lax.axis_index("expert")
    barrier = pltpu.get_barrier_semaphore()
    for k in range(1, 8):
        pl.semaphore_signal(barrier, inc=1, device_id=((bme + k) & 7, eme), device_id_type=MESH)
    scale = 1.0 / math.sqrt(HEAD)

    def copies(h):
        for k in range(1, 8):
            to = (bme + k) & 7
            yield pltpu.make_async_remote_copy(
                part.at[h, to], got.at[h, bme], ssem.at[h], rsem.at[h], device_id=(to, eme), device_id_type=MESH
            )

    for h in range(2):
        keys = k_ref[:, h * 128 : (h + 1) * 128]
        values = v_ref[:, h * 128 : (h + 1) * 128]
        kt[...] = keys.T
        vt[...] = values.T
        dk_acc[...] = jnp.zeros_like(dk_acc)
        dv_acc[...] = jnp.zeros_like(dv_acc)

        def tile(i, carry):
            t0 = pl.multiple_of(i * 16, 16)
            q = q_ref[pl.ds(t0, 16), h * 16 : (h + 1) * 16, :].reshape(256, 128)
            g = res_ref[pl.ds(t0, 16), h * 16 : (h + 1) * 16, :].reshape(256, 128)
            nt = (((1,), (1,)), ((), ()))
            scores = lax.dot_general(k_ref[:, h * 128 : (h + 1) * 128], q, nt, preferred_element_type=F32) * scale
            scores = jnp.where(posq_ref[pl.ds(i, 1), :] >= posk_ref[...], scores, -1e30)
            top = jnp.max(scores, axis=0, keepdims=True)
            weights = jnp.exp(scores - top)
            inverse = 1.0 / jnp.sum(weights, axis=0, keepdims=True)
            out = jnp.dot(vt[...], weights.astype(BF), preferred_element_type=F32) * inverse
            gt = g.astype(F32).T
            delta = jnp.sum(gt * out, axis=0, keepdims=True)
            probs = weights * inverse
            dv_acc[...] += jnp.dot(probs.astype(BF), g, preferred_element_type=F32)
            prob_grad = lax.dot_general(v_ref[:, h * 128 : (h + 1) * 128], g, nt, preferred_element_type=F32)
            score_grad = (probs * (prob_grad - delta)).astype(BF)
            dk_acc[...] += jnp.dot(score_grad, q, preferred_element_type=F32)
            dq = jnp.dot(kt[...], score_grad, preferred_element_type=F32) * scale
            dq_ref[pl.ds(t0, 16), h * 16 : (h + 1) * 16, :] = dq.T.astype(BF).reshape(16, 16, 128)
            return carry

        lax.fori_loop(0, 8, tile, 0)
        part[h, :, 0] = (dk_acc[...] * scale).astype(BF).reshape(8, 128, 128)
        part[h, :, 1] = dv_acc[...].astype(BF).reshape(8, 128, 128)
        got[h, bme] = part[h, bme]
        if h == 0:
            pl.semaphore_wait(barrier, 7)
        for copy in copies(h):
            copy.start()

    for h in range(2):
        seven = got.at[h, pl.ds(0, 7)]
        pltpu.make_async_copy(seven, seven, rsem.at[h]).wait()
        pltpu.make_async_copy(seven, seven, ssem.at[h]).wait()
        for t, out in ((0, dk_out), (1, dv_out)):
            total = got[h, 0, t].astype(F32)
            for s in range(1, 8):
                total += got[h, s, t].astype(F32)
            out[:, h * 128 : (h + 1) * 128] = total.astype(BF)


def attention(q3, res, keys, values, posq, posk):
    vmem = pl.BlockSpec(memory_space=pltpu.VMEM)
    return pl.pallas_call(
        attention_kernel,
        out_shape=(
            jax.ShapeDtypeStruct((128, 32, 128), BF),
            jax.ShapeDtypeStruct((128, 256), BF),
            jax.ShapeDtypeStruct((128, 256), BF),
        ),
        in_specs=[vmem] * 6,
        out_specs=(vmem,) * 3,
        scratch_shapes=[
            pltpu.VMEM((128, 1024), BF),
            pltpu.VMEM((128, 1024), BF),
            pltpu.VMEM((1024, 128), F32),
            pltpu.VMEM((1024, 128), F32),
            pltpu.VMEM((2, 8, 2, 128, 128), BF),
            pltpu.VMEM((2, 8, 2, 128, 128), BF),
            pltpu.SemaphoreType.DMA((2,)),
            pltpu.SemaphoreType.DMA((2,)),
        ],
        compiler_params=pltpu.CompilerParams(
            collective_id=1, has_side_effects=True, vmem_limit_bytes=40 << 20
        ),
    )(q3, res, keys, values, posq, posk)


def tables(ids):
    experts = jnp.arange(128, dtype=jnp.int32)
    match = ids[:, :, None] == experts
    named = jnp.any(match, axis=1)
    lower = (experts[:, None] > experts[None, :]).astype(BF)
    rank = jnp.dot(lower, named.astype(BF), preferred_element_type=F32).astype(jnp.int32)
    slots = jnp.arange(9, dtype=jnp.int32)
    hit = named[None] & (rank[None] == slots[:, None, None])
    tok = 128 + jnp.sum(jnp.where(hit, experts[None, :, None] - 128, 0), axis=1)
    tok = tok.reshape(3, 3, 4, 4, 4, 2)
    tok = jnp.stack(
        [
            tok[:, 0].transpose(0, 3, 1, 2, 4),
            tok[:, 1],
            tok[:, 2].transpose(0, 2, 3, 1, 4),
        ],
        axis=1,
    ).reshape(-1)
    slot = jnp.sum(jnp.where(match, rank[:, None, :], 0), axis=-1)
    y, z, x, c = ids // 32, (ids // 8) % 4, (ids // 2) % 4, ids % 2
    q = slot % 3
    place = jnp.where(
        q == 0,
        x * 32 + y * 8 + z * 2,
        jnp.where(q == 1, y * 32 + z * 8 + x * 2, z * 32 + x * 8 + y * 2),
    )
    ret = slot * 128 + place + c
    return tok, ret.reshape(-1)


def local(query, keys, values, grad_output, expert_ids, gate_weights, gate_up, down_weight, saved_preact, block_order):
    tok, ret = tables(expert_ids[0])
    g3 = jnp.pad(grad_output[0].reshape(128, 32, 128), ((0, 1), (0, 0), (0, 0)))
    s = saved_preact[0].reshape(4, 4, 4, 2, 3, 3, 1536)
    saved = jnp.stack(
        [
            s[..., 0, :].transpose(4, 1, 3, 0, 2, 5),
            s[..., 1, :].transpose(4, 2, 3, 1, 0, 5),
            s[..., 2, :].transpose(4, 0, 3, 2, 1, 5),
        ],
        axis=1,
    ).reshape(9, 128, 1536)
    res, kf, vf = exchange(
        tok, ret, gate_weights[0].reshape(-1), g3, keys[0], values[0], saved, down_weight[0], gate_up[0]
    )
    all_rows = jnp.arange(1024, dtype=jnp.int32)
    position = block_order[all_rows // 64] * 64 + all_rows % 64
    own = lax.dynamic_slice(position, (lax.axis_index("blk") * 128,), (128,))
    posq = jnp.repeat(own, 16).reshape(8, 256)
    dq, dk, dv = attention(
        query[0].reshape(128, 32, 128), res, kf.reshape(1024, 256), vf.reshape(1024, 256), posq, position[:, None]
    )
    return dq.reshape(1, 128, 4096), dk[None], dv[None]


def solution(mesh):
    token = P("expert", "blk", None)
    owner = P(("blk", "expert"), None, None)
    in_specs = (token,) * 6 + (owner, owner, P(("blk", "expert"), None, None, None), P())
    return jax.shard_map(local, mesh=mesh, in_specs=in_specs, out_specs=(token,) * 3, check_vma=False)
```

```python
import math

import jax
import jax.numpy as jnp
from jax import lax
from jax.experimental import pallas as pl
from jax.experimental.pallas import tpu as pltpu
from jax.sharding import PartitionSpec as P

MESH = pl.DeviceIdType.MESH
HEAD = 128
ORDERS = ((0, 1, 2), (1, 2, 0), (2, 0, 1))
BF = jnp.bfloat16
F32 = jnp.float32
GB = 256


def coords():
    b = lax.axis_index("blk")
    e = lax.axis_index("expert")
    return (e // 2) % 4, b // 2, (b % 2) * 2 + e // 8, e % 2


def device_of(x, y, z, c):
    return (y * 2 + z // 2, ((z % 2) * 4 + x) * 2 + c)


def place_expert(q, lane):
    a, b, d = ORDERS[q]
    t = [None] * 3
    t[a], t[b], t[d] = lane >> 5, (lane >> 3) & 3, (lane >> 1) & 3
    return t[1] * 32 + t[2] * 8 + t[0] * 2 + (lane & 1)


def exchange_kernel(
    ids_ref, wts_ref, g_ref, k_ref, v_ref, saved_ref, down_ref, gate_ref,
    res_ref, kf_ref, vf_ref,
    S, A, B, R, X, act, D, G, sv, acc, rank_ref, mix_ref, order_ref,
    ssem, rsem, lsem, kvs, kvr, dsem, gsem, svsem,
):
    x, y, z, c = coords()
    cc = (x, y, z)
    bme = lax.axis_index("blk")
    eme = lax.axis_index("expert")

    def dv(dim, v, core):
        t = [x, y, z]
        t[dim] = v
        return device_of(t[0], t[1], t[2], core)

    barrier = pltpu.get_barrier_semaphore()
    peers = [dv(dim, (cc[dim] + k) & 3, c ^ dc) for dim in range(3) for k in range(1, 4) for dc in range(2)]
    peers.append(dv(0, x, c ^ 1))
    peers += [device_of(x, (y + k) & 3, z ^ 2, c) for k in range(1, 4)]
    for p in peers:
        pl.semaphore_signal(barrier, inc=1, device_id=p, device_id_type=MESH)

    pltpu.make_async_copy(down_ref, D, dsem).start()

    def gate_copy(block, slot):
        return pltpu.make_async_copy(gate_ref.at[pl.ds(block * GB, GB)], G.at[slot], gsem.at[slot])

    gate_copy(0, 0).start()
    gate_copy(1, 1).start()

    sub = lax.broadcasted_iota(jnp.int32, (128, 128), 0)
    lane = lax.broadcasted_iota(jnp.int32, (128, 128), 1)
    upper_half = jnp.where(sub < lane, 1.0, 0.0).astype(BF)
    for q in range(3):
        expert = place_expert(q, sub)
        named = jnp.zeros((128, 128), F32)
        mix = jnp.zeros((128, 128), F32)
        for k in range(8):
            match = ids_ref[k : k + 1, :] == expert
            named += jnp.where(match, 1.0, 0.0)
            mix += jnp.where(match, wts_ref[k : k + 1, :], 0.0)
        rank = jnp.dot(named.astype(BF), upper_half, preferred_element_type=F32)
        rank_ref[q] = jnp.where(named > 0.5, rank, -1.0)
        mix_ref[q] = mix

    rows = lax.broadcasted_iota(jnp.int32, (256, 256), 0)
    cols = lax.broadcasted_iota(jnp.int32, (256, 256), 1)
    perm = jnp.where(cols == (rows & 15) * 16 + (rows >> 4), 1.0, 0.0).astype(BF)

    def unpacked(lo, hi, x0):
        out = jnp.dot(perm, jnp.concatenate([lo, hi], axis=1), preferred_element_type=F32).astype(BF)
        for u in range(16):
            X[pl.ds(x0, 16), u * 128 : (u + 1) * 128] = out[u * 16 : (u + 1) * 16, :128]
            X[pl.ds(x0, 16), 2048 + u * 128 : 2048 + (u + 1) * 128] = out[u * 16 : (u + 1) * 16, 128:]

    def packed(x0):
        lo = jnp.concatenate([X[pl.ds(x0, 16), u * 128 : (u + 1) * 128] for u in range(16)], axis=0)
        hi = jnp.concatenate([X[pl.ds(x0, 16), 2048 + u * 128 : 2048 + (u + 1) * 128] for u in range(16)], axis=0)
        return jnp.dot(perm, jnp.concatenate([lo, hi], axis=1), preferred_element_type=F32).astype(BF)

    def build(j):
        for q in range(3):
            pick = jnp.where(rank_ref[q] == float(3 * j + q), 1.0, 0.0).astype(BF)
            for h in range(4):
                X[q * 128 : (q + 1) * 128, h * 1024 : (h + 1) * 1024] = jnp.dot(
                    pick, g_ref[:, h * 1024 : (h + 1) * 1024], preferred_element_type=F32
                ).astype(BF)

        def body(i, carry):
            out = packed(pl.multiple_of(i * 16, 16))
            at = j * 12 + i // 2
            S[at, pl.ds(i % 2 * 2, 2), :, :16, :] = out[:, :128].reshape(2, 8, 16, 128)
            S[at, pl.ds(i % 2 * 2, 2), :, 16:, :] = out[:, 128:].reshape(2, 8, 16, 128)
            return carry

        lax.fori_loop(0, 24, body, 0)

    def combine(j):
        def body(i, carry):
            at = j * 12 + i // 2
            lo = S[at, pl.ds(i % 2 * 2, 2), :, :16, :].reshape(256, 128)
            hi = S[at, pl.ds(i % 2 * 2, 2), :, 16:, :].reshape(256, 128)
            unpacked(lo, hi, pl.multiple_of(i * 16, 16))
            return carry

        lax.fori_loop(0, 24, body, 0)
        mix = jnp.concatenate(
            [jnp.where(rank_ref[q] == float(3 * j + q), mix_ref[q], 0.0) for q in range(3)], axis=0
        ).T.astype(BF)
        for h in range(4):
            cut = slice(h * 1024, (h + 1) * 1024)
            before = g_ref[:, cut].astype(F32) if j == 0 else acc[:, cut]
            total = before + jnp.dot(mix, X[:, cut], preferred_element_type=F32)
            if j < 2:
                acc[:, cut] = total
            else:
                res_ref[:, cut] = total.astype(BF)

    def saved_copy(j):
        return pltpu.make_async_copy(saved_ref.at[pl.ds(3 * j, 3)], sv, svsem)

    saved_copy(0).start()

    for q in range(3):
        a, b, d = ORDERS[q]
        t = [None] * 3
        t[a], t[b], t[d] = sub & 3, (sub >> 2) & 3, sub >> 5
        source = t[1] * 32 + t[2] * 8 + t[0] * 2 + ((sub >> 4) & 1)
        order_ref[q] = jnp.where(lane == source, 1.0, 0.0).astype(BF)

    build(0)
    pl.semaphore_wait(barrier, len(peers))

    def remote(src, dst, ph, j, q, dev):
        return pltpu.make_async_remote_copy(
            src, dst, ssem.at[ph, j, q], rsem.at[ph, j, q], device_id=dev, device_id_type=MESH
        )

    def phase(ph, j, q):
        a, b, d = ORDERS[q]
        ma, mb, md = cc[a], cc[b], cc[d]
        n = 3 * j + q
        for k in (2, 1, 3, 0):
            if ph in (0, 5):
                v = (ma + k) & 3
                if ph == 0:
                    ops = [(S.at[n * 4 + v], A.at[n, ma], dv(a, v, c), k == 0)]
                else:
                    ops = [(A.at[n, v], S.at[n * 4 + ma], dv(a, v, c), k == 0)]
            elif ph in (1, 4):
                v = (mb + k) & 3
                if ph == 1:
                    ops = [(A.at[n, :, v], B.at[n, pl.ds(mb * 4, 4)], dv(b, v, c), k == 0)]
                else:
                    ops = [(B.at[n, pl.ds(v * 4, 4)], A.at[n, :, mb], dv(b, v, c), k == 0)]
            else:
                v = (md + k) & 3
                ops = []
                for dc in range(2):
                    t = c ^ dc
                    here = k == 0 and dc == 0
                    if ph == 2:
                        ops.append((B.at[n, :, v * 2 + t], R.at[n, pl.ds((md * 2 + c) * 16, 16)], dv(d, v, t), here))
                    else:
                        ops.append((R.at[n, pl.ds((v * 2 + t) * 16, 16)], B.at[n, :, md * 2 + c], dv(d, v, t), here))
            for src, dst, dev, here in ops:
                if here:
                    pltpu.make_async_copy(src, dst, lsem.at[ph, j, q]).start()
                else:
                    remote(src, dst, ph, j, q, dev).start()

    def wait(ph, j, q):
        mine = 16 if ph in (2, 3) else 32
        far = R.at[0, pl.ds(0, 128 - mine)]
        near = R.at[0, pl.ds(0, mine)]
        pltpu.make_async_copy(far, far, rsem.at[ph, j, q]).wait()
        pltpu.make_async_copy(near, near, lsem.at[ph, j, q]).wait()
        pltpu.make_async_copy(far, far, ssem.at[ph, j, q]).wait()

    def experts(j):
        def unpack(i, carry):
            n = 3 * j + i // 8
            r0 = pl.multiple_of((i % 8) * 16, 16)
            lo = R[n, pl.ds(r0, 16), :16, :].reshape(256, 128)
            hi = R[n, pl.ds(r0, 16), 16:, :].reshape(256, 128)
            unpacked(lo, hi, pl.multiple_of(i * 16, 16))
            return carry

        lax.fori_loop(0, 24, unpack, 0)
        if j == 0:
            pltpu.make_async_copy(down_ref, D, dsem).wait()

        def first(i, carry):
            at = pl.multiple_of(i * 256, 256)
            dg = lax.dot_general(
                X[...], D[pl.ds(at, 256), :], (((1,), (1,)), ((), ())), preferred_element_type=F32
            )
            for q in range(3):
                cut = slice(q * 128, (q + 1) * 128)
                gate = jnp.dot(order_ref[q], sv[q, :, pl.ds(at, 256)], preferred_element_type=F32)
                upper = jnp.dot(order_ref[q], sv[q, :, pl.ds(768 + at, 256)], preferred_element_type=F32)
                sigma = 1.0 / (1.0 + jnp.exp(-gate))
                ds = dg[cut] * sigma
                act[cut, pl.ds(at, 256)] = (ds * upper * (1.0 + gate * (1.0 - sigma))).astype(BF)
                act[cut, pl.ds(768 + at, 256)] = (ds * gate).astype(BF)
            return carry

        saved_copy(j).wait()
        lax.fori_loop(0, 3, first, 0)
        if j < 2:
            saved_copy(j + 1).start()
        blocks = 4096 // GB

        def second(i, carry):
            slot = i % 2
            gate_copy(i, slot).wait()
            at = pl.multiple_of(i * GB, GB)
            X[:, pl.ds(at, GB)] = lax.dot_general(
                act[...], G[slot], (((1,), (1,)), ((), ())), preferred_element_type=F32
            ).astype(BF)
            if j < 2:
                gate_copy((i + 2) % blocks, slot).start()
            else:
                @pl.when(i < blocks - 2)
                def _():
                    gate_copy(i + 2, slot).start()
            return carry

        lax.fori_loop(0, blocks, second, 0)

        def pack(i, carry):
            n = 3 * j + i // 8
            r0 = pl.multiple_of((i % 8) * 16, 16)
            out = packed(pl.multiple_of(i * 16, 16))
            R[n, pl.ds(r0, 16), :16, :] = out[:, :128].reshape(16, 16, 128)
            R[n, pl.ds(r0, 16), 16:, :] = out[:, 128:].reshape(16, 16, 128)
            return carry

        lax.fori_loop(0, 24, pack, 0)

    def each(ph, j):
        for q in range(3):
            phase(ph, j, q)

    def onward(ph, j):
        for q in range(3):
            wait(ph, j, q)
            if ph not in (2, 5):
                phase(ph + 1, j, q)

    each(0, 0)
    kf_ref[bme] = k_ref[...]
    vf_ref[bme] = v_ref[...]
    for k in range(1, 8):
        to = (bme + k) & 7
        for src, dst, t in ((k_ref, kf_ref, 0), (v_ref, vf_ref, 1)):
            pltpu.make_async_remote_copy(
                src, dst.at[bme], kvs.at[t], kvr.at[t], device_id=(to, eme), device_id_type=MESH
            ).start()
    build(1)
    onward(0, 0)
    each(0, 1)
    build(2)
    onward(1, 0)
    onward(0, 1)
    each(0, 2)
    onward(2, 0)
    onward(1, 1)
    onward(0, 2)
    experts(0)
    onward(2, 1)
    onward(1, 2)
    each(3, 0)
    experts(1)
    onward(3, 0)
    onward(2, 2)
    each(3, 1)
    experts(2)
    onward(4, 0)
    onward(3, 1)
    each(3, 2)
    onward(5, 0)
    combine(0)
    onward(4, 1)
    onward(3, 2)
    onward(4, 2)
    onward(5, 1)
    combine(1)
    onward(5, 2)
    combine(2)

    for t, full in ((0, kf_ref), (1, vf_ref)):
        seven = full.at[pl.ds(0, 7)]
        pltpu.make_async_copy(seven, seven, kvr.at[t]).wait()
        pltpu.make_async_copy(seven, seven, kvs.at[t]).wait()


def exchange(ids, wts, g, keys, values, saved, down, gate):
    vmem = pl.BlockSpec(memory_space=pltpu.VMEM)
    hbm = pl.BlockSpec(memory_space=pl.ANY)
    row = (32, 128)
    return pl.pallas_call(
        exchange_kernel,
        out_shape=(
            jax.ShapeDtypeStruct((128, 4096), BF),
            jax.ShapeDtypeStruct((8, 128, 256), BF),
            jax.ShapeDtypeStruct((8, 128, 256), BF),
        ),
        in_specs=[vmem] * 5 + [hbm] * 3,
        out_specs=(vmem, vmem, vmem),
        scratch_shapes=[
            pltpu.VMEM((36, 4, 8) + row, BF),
            pltpu.VMEM((9, 4, 4, 8) + row, BF),
            pltpu.VMEM((9, 16, 8) + row, BF),
            pltpu.VMEM((9, 128) + row, BF),
            pltpu.VMEM((384, 4096), BF),
            pltpu.VMEM((384, 1536), BF),
            pltpu.VMEM((768, 4096), BF),
            pltpu.VMEM((2, GB, 1536), BF),
            pltpu.VMEM((3, 128, 1536), BF),
            pltpu.VMEM((128, 4096), F32),
            pltpu.VMEM((3, 128, 128), F32),
            pltpu.VMEM((3, 128, 128), F32),
            pltpu.VMEM((3, 128, 128), BF),
            pltpu.SemaphoreType.DMA((6, 3, 3)),
            pltpu.SemaphoreType.DMA((6, 3, 3)),
            pltpu.SemaphoreType.DMA((6, 3, 3)),
            pltpu.SemaphoreType.DMA((2,)),
            pltpu.SemaphoreType.DMA((2,)),
            pltpu.SemaphoreType.DMA,
            pltpu.SemaphoreType.DMA((2,)),
            pltpu.SemaphoreType.DMA,
        ],
        compiler_params=pltpu.CompilerParams(
            collective_id=0, has_side_effects=True, vmem_limit_bytes=63 << 20
        ),
    )(ids, wts, g, keys, values, saved, down, gate)


def attention_kernel(
    order_ref, q_ref, res_ref, k_ref, v_ref,
    dq_ref, dk_out, dv_out,
    posk_ref, kt, vt, dk_acc, dv_acc, part, got, ssem, rsem,
):
    bme = lax.axis_index("blk")
    eme = lax.axis_index("expert")
    barrier = pltpu.get_barrier_semaphore()
    for k in range(1, 8):
        pl.semaphore_signal(barrier, inc=1, device_id=((bme + k) & 7, eme), device_id_type=MESH)
    scale = 1.0 / math.sqrt(HEAD)
    within = lax.broadcasted_iota(jnp.int32, (64, 1), 0)
    for i in range(16):
        posk_ref[i * 64 : (i + 1) * 64, :] = order_ref[i] * 64 + within
    lanes = lax.broadcasted_iota(jnp.int32, (1, 256), 1) & 127
    posq = jnp.where(lanes < 64, order_ref[2 * bme] * 64, order_ref[2 * bme + 1] * 64) + (lanes & 63)

    def copies(h):
        for k in range(1, 8):
            to = (bme + k) & 7
            yield pltpu.make_async_remote_copy(
                part.at[h, to], got.at[h, bme], ssem.at[h], rsem.at[h], device_id=(to, eme), device_id_type=MESH
            )

    for h in range(2):
        keys = k_ref[:, h * 128 : (h + 1) * 128]
        values = v_ref[:, h * 128 : (h + 1) * 128]
        kt[...] = keys.T
        vt[...] = values.T
        dk_acc[...] = jnp.zeros_like(dk_acc)
        dv_acc[...] = jnp.zeros_like(dv_acc)

        def tile(i, carry):
            one = pl.ds(pl.multiple_of((h * 16 + 2 * i) * 128, 128), 128)
            two = pl.ds(pl.multiple_of((h * 16 + 2 * i + 1) * 128, 128), 128)
            q = jnp.concatenate([q_ref[:, one], q_ref[:, two]], axis=0)
            g = jnp.concatenate([res_ref[:, one], res_ref[:, two]], axis=0)
            nt = (((1,), (1,)), ((), ()))
            scores = lax.dot_general(k_ref[:, h * 128 : (h + 1) * 128], q, nt, preferred_element_type=F32) * scale
            scores = jnp.where(posq >= posk_ref[...], scores, -1e30)
            top = jnp.max(scores, axis=0, keepdims=True)
            weights = jnp.exp(scores - top)
            inverse = 1.0 / jnp.sum(weights, axis=0, keepdims=True)
            out = jnp.dot(vt[...], weights.astype(BF), preferred_element_type=F32) * inverse
            delta = jnp.sum(g.astype(F32).T * out, axis=0, keepdims=True)
            probs = weights * inverse
            dv_acc[...] += jnp.dot(probs.astype(BF), g, preferred_element_type=F32)
            prob_grad = lax.dot_general(v_ref[:, h * 128 : (h + 1) * 128], g, nt, preferred_element_type=F32)
            score_grad = (probs * (prob_grad - delta)).astype(BF)
            dk_acc[...] += jnp.dot(score_grad, q, preferred_element_type=F32)
            dq = (jnp.dot(kt[...], score_grad, preferred_element_type=F32) * scale).T.astype(BF)
            dq_ref[:, one] = dq[:128]
            dq_ref[:, two] = dq[128:]
            return carry

        lax.fori_loop(0, 8, tile, 0)
        part[h, :, 0] = (dk_acc[...] * scale).astype(BF).reshape(8, 128, 128)
        part[h, :, 1] = dv_acc[...].astype(BF).reshape(8, 128, 128)
        got[h, bme] = part[h, bme]
        if h == 0:
            pl.semaphore_wait(barrier, 7)
        for copy in copies(h):
            copy.start()

    for h in range(2):
        seven = got.at[h, pl.ds(0, 7)]
        pltpu.make_async_copy(seven, seven, rsem.at[h]).wait()
        pltpu.make_async_copy(seven, seven, ssem.at[h]).wait()
        for t, out in ((0, dk_out), (1, dv_out)):
            total = got[h, 0, t].astype(F32)
            for s in range(1, 8):
                total += got[h, s, t].astype(F32)
            out[:, h * 128 : (h + 1) * 128] = total.astype(BF)


def attention(order, query, res, keys, values):
    vmem = pl.BlockSpec(memory_space=pltpu.VMEM)
    return pl.pallas_call(
        attention_kernel,
        out_shape=(
            jax.ShapeDtypeStruct((128, 4096), BF),
            jax.ShapeDtypeStruct((128, 256), BF),
            jax.ShapeDtypeStruct((128, 256), BF),
        ),
        in_specs=[pl.BlockSpec(memory_space=pltpu.SMEM)] + [vmem] * 4,
        out_specs=(vmem,) * 3,
        scratch_shapes=[
            pltpu.VMEM((1024, 1), jnp.int32),
            pltpu.VMEM((128, 1024), BF),
            pltpu.VMEM((128, 1024), BF),
            pltpu.VMEM((1024, 128), F32),
            pltpu.VMEM((1024, 128), F32),
            pltpu.VMEM((2, 8, 2, 128, 128), BF),
            pltpu.VMEM((2, 8, 2, 128, 128), BF),
            pltpu.SemaphoreType.DMA((2,)),
            pltpu.SemaphoreType.DMA((2,)),
        ],
        compiler_params=pltpu.CompilerParams(
            collective_id=1, has_side_effects=True, vmem_limit_bytes=40 << 20
        ),
    )(order, query, res, keys, values)


def local(query, keys, values, grad_output, expert_ids, gate_weights, gate_up, down_weight, saved_preact, block_order):
    res, kf, vf = exchange(
        expert_ids[0].T,
        gate_weights[0].T,
        grad_output[0],
        keys[0],
        values[0],
        saved_preact[0].transpose(1, 0, 2),
        down_weight[0],
        gate_up[0],
    )
    dq, dk, dv = attention(block_order, query[0], res, kf.reshape(1024, 256), vf.reshape(1024, 256))
    return dq[None], dk[None], dv[None]


def solution(mesh):
    token = P("expert", "blk", None)
    owner = P(("blk", "expert"), None, None)
    in_specs = (token,) * 6 + (owner, owner, P(("blk", "expert"), None, None, None), P())
    return jax.shard_map(local, mesh=mesh, in_specs=in_specs, out_specs=(token,) * 3, check_vma=False)
```

```python
import math

import jax
import jax.numpy as jnp
from jax import lax
from jax.experimental import pallas as pl
from jax.experimental.pallas import tpu as pltpu
from jax.sharding import PartitionSpec as P

MESH = pl.DeviceIdType.MESH
HEAD = 128
ORDERS = ((0, 1, 2), (1, 2, 0), (2, 0, 1))
BF = jnp.bfloat16
F32 = jnp.float32
GB = 256


def coords():
    b = lax.axis_index("blk")
    e = lax.axis_index("expert")
    return (e // 2) % 4, b // 2, (b % 2) * 2 + e // 8, e % 2


def device_of(x, y, z, c):
    return (y * 2 + z // 2, ((z % 2) * 4 + x) * 2 + c)


def place_expert(q, lane):
    a, b, d = ORDERS[q]
    t = [None] * 3
    t[a], t[b], t[d] = lane >> 5, (lane >> 3) & 3, (lane >> 1) & 3
    return t[1] * 32 + t[2] * 8 + t[0] * 2 + (lane & 1)


def exchange_kernel(
    block_ref, ids_ref, wts_ref, g_ref, q_ref, k_ref, v_ref, saved_ref, down_ref, gate_ref,
    dq_ref, dk_out, dv_out,
    S, A, B, R, X, act, D, G, sv, acc, rank_ref, mix_ref, order_ref,
    kf_ref, vf_ref, kt, vt, posk_ref, fwd_out, log_total, dk_acc, dv_acc,
    ssem, rsem, lsem, kvs, kvr, dsem, gsem, svsem, pairs, pairr, outsem,
):
    x, y, z, c = coords()
    cc = (x, y, z)
    bme = lax.axis_index("blk")
    eme = lax.axis_index("expert")

    def dv(dim, v, core):
        t = [x, y, z]
        t[dim] = v
        return device_of(t[0], t[1], t[2], core)

    barrier = pltpu.get_barrier_semaphore()
    peers = [dv(dim, (cc[dim] + k) & 3, c ^ dc) for dim in range(3) for k in range(1, 4) for dc in range(2)]
    peers.append(dv(0, x, c ^ 1))
    peers += [device_of(x, (y + k) & 3, z ^ 2, c) for k in range(1, 4)]
    for p in peers:
        pl.semaphore_signal(barrier, inc=1, device_id=p, device_id_type=MESH)

    pltpu.make_async_copy(down_ref, D, dsem).start()

    def gate_copy(block, slot):
        return pltpu.make_async_copy(gate_ref.at[pl.ds(block * GB, GB)], G.at[slot], gsem.at[slot])

    gate_copy(0, 0).start()
    gate_copy(1, 1).start()

    sub = lax.broadcasted_iota(jnp.int32, (128, 128), 0)
    lane = lax.broadcasted_iota(jnp.int32, (128, 128), 1)
    upper_half = jnp.where(sub < lane, 1.0, 0.0).astype(BF)
    for q in range(3):
        expert = place_expert(q, sub)
        named = jnp.zeros((128, 128), F32)
        mix = jnp.zeros((128, 128), F32)
        for k in range(8):
            match = ids_ref[k : k + 1, :] == expert
            named += jnp.where(match, 1.0, 0.0)
            mix += jnp.where(match, wts_ref[k : k + 1, :], 0.0)
        rank = jnp.dot(named.astype(BF), upper_half, preferred_element_type=F32)
        rank_ref[q] = jnp.where(named > 0.5, rank, -1.0)
        mix_ref[q] = mix

    rows = lax.broadcasted_iota(jnp.int32, (256, 256), 0)
    cols = lax.broadcasted_iota(jnp.int32, (256, 256), 1)
    perm = jnp.where(cols == (rows & 15) * 16 + (rows >> 4), 1.0, 0.0).astype(BF)

    def unpacked(lo, hi, x0):
        out = jnp.dot(perm, jnp.concatenate([lo, hi], axis=1), preferred_element_type=F32).astype(BF)
        for u in range(16):
            X[pl.ds(x0, 16), u * 128 : (u + 1) * 128] = out[u * 16 : (u + 1) * 16, :128]
            X[pl.ds(x0, 16), 2048 + u * 128 : 2048 + (u + 1) * 128] = out[u * 16 : (u + 1) * 16, 128:]

    def packed(x0):
        lo = jnp.concatenate([X[pl.ds(x0, 16), u * 128 : (u + 1) * 128] for u in range(16)], axis=0)
        hi = jnp.concatenate([X[pl.ds(x0, 16), 2048 + u * 128 : 2048 + (u + 1) * 128] for u in range(16)], axis=0)
        return jnp.dot(perm, jnp.concatenate([lo, hi], axis=1), preferred_element_type=F32).astype(BF)

    def build(j):
        for q in range(3):
            pick = jnp.where(rank_ref[q] == float(3 * j + q), 1.0, 0.0).astype(BF)
            for h in range(4):
                X[q * 128 : (q + 1) * 128, h * 1024 : (h + 1) * 1024] = jnp.dot(
                    pick, g_ref[:, h * 1024 : (h + 1) * 1024], preferred_element_type=F32
                ).astype(BF)

        def body(i, carry):
            out = packed(pl.multiple_of(i * 16, 16))
            at = j * 12 + i // 2
            S[at, pl.ds(i % 2 * 2, 2), :, :16, :] = out[:, :128].reshape(2, 8, 16, 128)
            S[at, pl.ds(i % 2 * 2, 2), :, 16:, :] = out[:, 128:].reshape(2, 8, 16, 128)
            return carry

        lax.fori_loop(0, 24, body, 0)

    def combine(j, halves=(0, 1)):
        if len(halves) == 2:
            def body(i, carry):
                at = j * 12 + i // 2
                lo = S[at, pl.ds(i % 2 * 2, 2), :, :16, :].reshape(256, 128)
                hi = S[at, pl.ds(i % 2 * 2, 2), :, 16:, :].reshape(256, 128)
                unpacked(lo, hi, pl.multiple_of(i * 16, 16))
                return carry

            lax.fori_loop(0, 24, body, 0)
        else:
            half = halves[0]

            def body(i, carry):
                at = j * 12 + i
                x0 = pl.multiple_of(i * 32, 32)
                lo = S[at, :2, :, half * 16 : half * 16 + 16, :].reshape(256, 128)
                hi = S[at, 2:, :, half * 16 : half * 16 + 16, :].reshape(256, 128)
                out = jnp.dot(perm, jnp.concatenate([lo, hi], axis=1), preferred_element_type=F32).astype(BF)
                for u in range(16):
                    to = slice(half * 2048 + u * 128, half * 2048 + (u + 1) * 128)
                    X[pl.ds(x0, 16), to] = out[u * 16 : (u + 1) * 16, :128]
                    X[pl.ds(x0 + 16, 16), to] = out[u * 16 : (u + 1) * 16, 128:]
                return carry

            lax.fori_loop(0, 12, body, 0)
        mix = jnp.concatenate(
            [jnp.where(rank_ref[q] == float(3 * j + q), mix_ref[q], 0.0) for q in range(3)], axis=0
        ).T.astype(BF)
        for half in halves:
            for h in (2 * half, 2 * half + 1):
                cut = slice(h * 1024, (h + 1) * 1024)
                before = g_ref[:, cut].astype(F32) if j == 0 else acc[:, cut]
                total = before + jnp.dot(mix, X[:, cut], preferred_element_type=F32)
                if j < 2:
                    acc[:, cut] = total
                else:
                    D[:128, cut] = total.astype(BF)

    def saved_copy(j):
        return pltpu.make_async_copy(saved_ref.at[pl.ds(3 * j, 3)], sv, svsem)

    saved_copy(0).start()

    for q in range(3):
        a, b, d = ORDERS[q]
        t = [None] * 3
        t[a], t[b], t[d] = sub & 3, (sub >> 2) & 3, sub >> 5
        source = t[1] * 32 + t[2] * 8 + t[0] * 2 + ((sub >> 4) & 1)
        order_ref[q] = jnp.where(lane == source, 1.0, 0.0).astype(BF)

    build(0)
    pl.semaphore_wait(barrier, len(peers))

    def remote(src, dst, ph, j, q, dev):
        return pltpu.make_async_remote_copy(
            src, dst, ssem.at[ph, j, q], rsem.at[ph, j, q], device_id=dev, device_id_type=MESH
        )

    def phase(ph, j, q, half=None):
        a, b, d = ORDERS[q]
        ma, mb, md = cc[a], cc[b], cc[d]
        n = 3 * j + q
        for k in (2, 1, 3, 0):
            if ph in (0, 5):
                v = (ma + k) & 3
                if ph == 0:
                    ops = [(S.at[n * 4 + v], A.at[n, ma], dv(a, v, c), k == 0)]
                else:
                    ops = [(A.at[n, v], S.at[n * 4 + ma], dv(a, v, c), k == 0)]
            elif ph in (1, 4):
                v = (mb + k) & 3
                if ph == 1:
                    ops = [(A.at[n, :, v], B.at[n, pl.ds(mb * 4, 4)], dv(b, v, c), k == 0)]
                else:
                    ops = [(B.at[n, pl.ds(v * 4, 4)], A.at[n, :, mb], dv(b, v, c), k == 0)]
            else:
                v = (md + k) & 3
                ops = []
                for dc in range(2):
                    t = c ^ dc
                    here = k == 0 and dc == 0
                    if ph == 2:
                        ops.append((B.at[n, :, v * 2 + t], R.at[n, pl.ds((md * 2 + c) * 16, 16)], dv(d, v, t), here))
                    else:
                        ops.append((R.at[n, pl.ds((v * 2 + t) * 16, 16)], B.at[n, :, md * 2 + c], dv(d, v, t), here))
            at = j + (half or 0)
            for src, dst, dev, here in ops:
                if half is not None:
                    cut = (slice(None),) * (len(src.shape) - 2) + (pl.ds(half * 16, 16),)
                    src, dst = src.at[cut], dst.at[cut]
                if here:
                    pltpu.make_async_copy(src, dst, lsem.at[ph, at, q]).start()
                else:
                    remote(src, dst, ph, at, q, dev).start()

    def wait(ph, j, q, half=None):
        mine = 16 if ph in (2, 3) else 32
        deep = pl.ds(0, 32 if half is None else 16)
        at = j + (half or 0)
        far = R.at[0, pl.ds(0, 128 - mine), deep]
        near = R.at[0, pl.ds(0, mine), deep]
        pltpu.make_async_copy(far, far, rsem.at[ph, at, q]).wait()
        pltpu.make_async_copy(near, near, lsem.at[ph, at, q]).wait()
        pltpu.make_async_copy(far, far, ssem.at[ph, at, q]).wait()

    def experts(j):
        def unpack(i, carry):
            n = 3 * j + i // 8
            r0 = pl.multiple_of((i % 8) * 16, 16)
            lo = R[n, pl.ds(r0, 16), :16, :].reshape(256, 128)
            hi = R[n, pl.ds(r0, 16), 16:, :].reshape(256, 128)
            unpacked(lo, hi, pl.multiple_of(i * 16, 16))
            return carry

        lax.fori_loop(0, 24, unpack, 0)
        if j == 0:
            pltpu.make_async_copy(down_ref, D, dsem).wait()

        def first(i, carry):
            at = pl.multiple_of(i * 256, 256)
            dg = lax.dot_general(
                X[...], D[pl.ds(at, 256), :], (((1,), (1,)), ((), ())), preferred_element_type=F32
            )
            for q in range(3):
                cut = slice(q * 128, (q + 1) * 128)
                gate = jnp.dot(order_ref[q], sv[q, :, pl.ds(at, 256)], preferred_element_type=F32)
                upper = jnp.dot(order_ref[q], sv[q, :, pl.ds(768 + at, 256)], preferred_element_type=F32)
                sigma = 1.0 / (1.0 + jnp.exp(-gate))
                ds = dg[cut] * sigma
                act[cut, pl.ds(at, 256)] = (ds * upper * (1.0 + gate * (1.0 - sigma))).astype(BF)
                act[cut, pl.ds(768 + at, 256)] = (ds * gate).astype(BF)
            return carry

        saved_copy(j).wait()
        lax.fori_loop(0, 3, first, 0)
        if j < 2:
            saved_copy(j + 1).start()
        blocks = 4096 // GB

        def second(i, carry):
            slot = i % 2
            gate_copy(i, slot).wait()
            at = pl.multiple_of(i * GB, GB)
            X[:, pl.ds(at, GB)] = lax.dot_general(
                act[...], G[slot], (((1,), (1,)), ((), ())), preferred_element_type=F32
            ).astype(BF)
            if j < 2:
                gate_copy((i + 2) % blocks, slot).start()
            else:
                @pl.when(i < blocks - 2)
                def _():
                    gate_copy(i + 2, slot).start()
            return carry

        lax.fori_loop(0, blocks, second, 0)

        def pack(i, carry):
            n = 3 * j + i // 8
            r0 = pl.multiple_of((i % 8) * 16, 16)
            out = packed(pl.multiple_of(i * 16, 16))
            R[n, pl.ds(r0, 16), :16, :] = out[:, :128].reshape(16, 16, 128)
            R[n, pl.ds(r0, 16), 16:, :] = out[:, 128:].reshape(16, 16, 128)
            return carry

        lax.fori_loop(0, 24, pack, 0)

    def each(ph, j, half=None):
        for q in range(3):
            phase(ph, j, q, half)

    def onward(ph, j, half=None):
        for q in range(3):
            wait(ph, j, q, half)
            if ph not in (2, 5):
                phase(ph + 1, j, q, half)

    scale = 1.0 / math.sqrt(HEAD)
    nt = (((1,), (1,)), ((), ()))
    within = lax.broadcasted_iota(jnp.int32, (64, 1), 0)
    for i in range(16):
        posk_ref[i * 64 : (i + 1) * 64, :] = block_ref[i] * 64 + within
    token = lax.broadcasted_iota(jnp.int32, (1, 256), 1) & 127
    posq = jnp.where(token < 64, block_ref[2 * bme] * 64, block_ref[2 * bme + 1] * 64) + (token & 63)

    def two_heads(ref, top, h, i):
        one = pl.ds(pl.multiple_of((h * 16 + 2 * i) * 128, 128), 128)
        two = pl.ds(pl.multiple_of((h * 16 + 2 * i + 1) * 128, 128), 128)
        return jnp.concatenate([ref[top : top + 128, one], ref[top : top + 128, two]], axis=0)

    def scores_of(h, q):
        keys = kf_ref[:, :, h * 128 : (h + 1) * 128].reshape(1024, 128)
        scores = lax.dot_general(keys, q, nt, preferred_element_type=F32) * scale
        return jnp.where(posq >= posk_ref[...], scores, -1e30)

    def attention_forward(h):
        kt[h] = kf_ref[:, :, h * 128 : (h + 1) * 128].reshape(1024, 128).T
        vt[h] = vf_ref[:, :, h * 128 : (h + 1) * 128].reshape(1024, 128).T

        def tile(i, carry):
            scores = scores_of(h, two_heads(q_ref, 0, h, i))
            top = jnp.max(scores, axis=0, keepdims=True)
            weights = jnp.exp(scores - top)
            total = jnp.sum(weights, axis=0, keepdims=True)
            out = jnp.dot(vt[h], weights.astype(BF), preferred_element_type=F32) / total
            fwd_out[h * 8 + i] = out.astype(BF)
            log_total[h * 8 + i] = top + jnp.log(total)
            return carry

        lax.fori_loop(0, 8, tile, 0)

    def pair_copies(h):
        rows = pl.ds(256 + 128 * h, 128)
        for k in range(1, 8):
            to = (bme + k) & 7
            yield pltpu.make_async_remote_copy(
                D.at[rows, pl.ds(pl.multiple_of(to * 256, 256), 256)],
                D.at[rows, pl.ds(pl.multiple_of(2048 + bme * 256, 256), 256)],
                pairs.at[h], pairr.at[h], device_id=(to, eme), device_id_type=MESH,
            )

    def query_copy(h):
        cols = pl.ds(h * 2048, 2048)
        return pltpu.make_async_copy(D.at[pl.ds(128, 128), cols], dq_ref.at[:, cols], outsem.at[h])

    def attention_backward(h):
        dk_acc[...] = jnp.zeros_like(dk_acc)
        dv_acc[...] = jnp.zeros_like(dv_acc)

        def tile(i, carry):
            q = two_heads(q_ref, 0, h, i)
            g = two_heads(D, 0, h, i)
            delta = jnp.sum(g.astype(F32).T * fwd_out[h * 8 + i].astype(F32), axis=0, keepdims=True)
            values = vf_ref[:, :, h * 128 : (h + 1) * 128].reshape(1024, 128)
            prob_grad = lax.dot_general(values, g, nt, preferred_element_type=F32)
            probs = jnp.exp(scores_of(h, q) - log_total[h * 8 + i])
            dv_acc[...] += jnp.dot(probs.astype(BF), g, preferred_element_type=F32)
            score_grad = (probs * (prob_grad - delta)).astype(BF)
            dk_acc[...] += jnp.dot(score_grad, q, preferred_element_type=F32)
            dq = (jnp.dot(kt[h], score_grad, preferred_element_type=F32) * scale).T.astype(BF)
            D[128:256, pl.ds(pl.multiple_of((h * 16 + 2 * i) * 128, 128), 128)] = dq[:128]
            D[128:256, pl.ds(pl.multiple_of((h * 16 + 2 * i + 1) * 128, 128), 128)] = dq[128:]
            return carry

        lax.fori_loop(0, 8, tile, 0)
        query_copy(h).start()
        rows = slice(256 + 128 * h, 384 + 128 * h)
        for b in range(8):
            D[rows, b * 256 : b * 256 + 128] = (dk_acc[b * 128 : (b + 1) * 128, :] * scale).astype(BF)
            D[rows, b * 256 + 128 : b * 256 + 256] = dv_acc[b * 128 : (b + 1) * 128, :].astype(BF)
        for copy in pair_copies(h):
            copy.start()
        D[rows, pl.ds(pl.multiple_of(2048 + bme * 256, 256), 256)] = D[
            rows, pl.ds(pl.multiple_of(bme * 256, 256), 256)
        ]

    def pair_sums(h):
        rows = slice(256 + 128 * h, 384 + 128 * h)
        seven = D.at[pl.ds(256 + 128 * h, 128), pl.ds(0, 1792)]
        pltpu.make_async_copy(seven, seven, pairr.at[h]).wait()
        pltpu.make_async_copy(seven, seven, pairs.at[h]).wait()
        total = D[rows, 2048:2304].astype(F32)
        for b in range(1, 8):
            total += D[rows, 2048 + b * 256 : 2304 + b * 256].astype(F32)
        dk_out[:, h * 128 : (h + 1) * 128] = total[:, :128].astype(BF)
        dv_out[:, h * 128 : (h + 1) * 128] = total[:, 128:].astype(BF)

    each(0, 0)
    kf_ref[bme] = k_ref[...]
    vf_ref[bme] = v_ref[...]
    for k in range(1, 8):
        to = (bme + k) & 7
        for src, dst, t in ((k_ref, kf_ref, 0), (v_ref, vf_ref, 1)):
            pltpu.make_async_remote_copy(
                src, dst.at[bme], kvs.at[t], kvr.at[t], device_id=(to, eme), device_id_type=MESH
            ).start()
    build(1)
    onward(0, 0)
    each(0, 1)
    build(2)
    for t, full in ((0, kf_ref), (1, vf_ref)):
        seven = full.at[pl.ds(0, 7)]
        pltpu.make_async_copy(seven, seven, kvr.at[t]).wait()
        pltpu.make_async_copy(seven, seven, kvs.at[t]).wait()
    attention_forward(0)
    onward(1, 0)
    onward(0, 1)
    each(0, 2)
    attention_forward(1)
    onward(2, 0)
    onward(1, 1)
    onward(0, 2)
    experts(0)
    onward(2, 1)
    onward(1, 2)
    each(3, 0)
    experts(1)
    onward(3, 0)
    onward(2, 2)
    each(3, 1)
    experts(2)
    onward(4, 0)
    onward(3, 1)
    each(3, 2, 0)
    each(3, 2, 1)
    onward(5, 0)
    combine(0)
    onward(4, 1)
    onward(3, 2, 0)
    onward(3, 2, 1)
    onward(5, 1)
    combine(1)
    onward(4, 2, 0)
    onward(4, 2, 1)
    onward(5, 2, 0)
    combine(2, (0,))
    attention_backward(0)
    onward(5, 2, 1)
    combine(2, (1,))
    attention_backward(1)
    pair_sums(0)
    pair_sums(1)
    query_copy(0).wait()
    query_copy(1).wait()


def exchange(order, ids, wts, g, query, keys, values, saved, down, gate):
    smem = pl.BlockSpec(memory_space=pltpu.SMEM)
    vmem = pl.BlockSpec(memory_space=pltpu.VMEM)
    hbm = pl.BlockSpec(memory_space=pl.ANY)
    row = (32, 128)
    return pl.pallas_call(
        exchange_kernel,
        out_shape=(
            jax.ShapeDtypeStruct((128, 4096), BF),
            jax.ShapeDtypeStruct((128, 256), BF),
            jax.ShapeDtypeStruct((128, 256), BF),
        ),
        in_specs=[smem] + [vmem] * 6 + [hbm] * 3,
        out_specs=(hbm, vmem, vmem),
        scratch_shapes=[
            pltpu.VMEM((36, 4, 8) + row, BF),
            pltpu.VMEM((9, 4, 4, 8) + row, BF),
            pltpu.VMEM((9, 16, 8) + row, BF),
            pltpu.VMEM((9, 128) + row, BF),
            pltpu.VMEM((384, 4096), BF),
            pltpu.VMEM((384, 1536), BF),
            pltpu.VMEM((768, 4096), BF),
            pltpu.VMEM((2, GB, 1536), BF),
            pltpu.VMEM((3, 128, 1536), BF),
            pltpu.VMEM((128, 4096), F32),
            pltpu.VMEM((3, 128, 128), F32),
            pltpu.VMEM((3, 128, 128), F32),
            pltpu.VMEM((3, 128, 128), BF),
            pltpu.VMEM((8, 128, 256), BF),
            pltpu.VMEM((8, 128, 256), BF),
            pltpu.VMEM((2, 128, 1024), BF),
            pltpu.VMEM((2, 128, 1024), BF),
            pltpu.VMEM((1024, 1), jnp.int32),
            pltpu.VMEM((16, 128, 256), BF),
            pltpu.VMEM((16, 1, 256), F32),
            pltpu.VMEM((1024, 128), F32),
            pltpu.VMEM((1024, 128), F32),
            pltpu.SemaphoreType.DMA((6, 4, 3)),
            pltpu.SemaphoreType.DMA((6, 4, 3)),
            pltpu.SemaphoreType.DMA((6, 4, 3)),
            pltpu.SemaphoreType.DMA((2,)),
            pltpu.SemaphoreType.DMA((2,)),
            pltpu.SemaphoreType.DMA,
            pltpu.SemaphoreType.DMA((2,)),
            pltpu.SemaphoreType.DMA,
            pltpu.SemaphoreType.DMA((2,)),
            pltpu.SemaphoreType.DMA((2,)),
            pltpu.SemaphoreType.DMA((2,)),
        ],
        compiler_params=pltpu.CompilerParams(
            collective_id=0, has_side_effects=True, vmem_limit_bytes=63 << 20
        ),
    )(order, ids, wts, g, query, keys, values, saved, down, gate)


def local(query, keys, values, grad_output, expert_ids, gate_weights, gate_up, down_weight, saved_preact, block_order):
    dq, dk, dv = exchange(
        block_order,
        expert_ids[0].T,
        gate_weights[0].T,
        grad_output[0],
        query[0],
        keys[0],
        values[0],
        saved_preact[0].transpose(1, 0, 2),
        down_weight[0],
        gate_up[0],
    )
    return dq[None], dk[None], dv[None]


def solution(mesh):
    token = P("expert", "blk", None)
    owner = P(("blk", "expert"), None, None)
    in_specs = (token,) * 6 + (owner, owner, P(("blk", "expert"), None, None, None), P())
    return jax.shard_map(local, mesh=mesh, in_specs=in_specs, out_specs=(token,) * 3, check_vma=False)
```

```python
import math

import jax
import jax.numpy as jnp
from jax import lax
from jax.experimental import pallas as pl
from jax.experimental.pallas import tpu as pltpu
from jax.sharding import PartitionSpec as P

MESH = pl.DeviceIdType.MESH
HEAD = 128
ORDERS = ((0, 1, 2), (1, 2, 0), (2, 0, 1))
BF = jnp.bfloat16
F32 = jnp.float32
GB = 256


def coords():
    b = lax.axis_index("blk")
    e = lax.axis_index("expert")
    return (e // 2) % 4, b // 2, (b % 2) * 2 + e // 8, e % 2


def device_of(x, y, z, c):
    return (y * 2 + z // 2, ((z % 2) * 4 + x) * 2 + c)


def place_expert(q, lane):
    a, b, d = ORDERS[q]
    t = [None] * 3
    t[a], t[b], t[d] = lane >> 5, (lane >> 3) & 3, (lane >> 1) & 3
    return t[1] * 32 + t[2] * 8 + t[0] * 2 + (lane & 1)


def exchange_kernel(
    block_ref, ids_ref, wts_ref, g_ref, q_ref, k_ref, v_ref, saved_ref, down_ref, gate_ref,
    dq_ref, dk_out, dv_out,
    S, A, B, R, X, act, D, G, sv, acc, rank_ref, mix_ref, order_ref,
    kf_ref, vf_ref, kt, vt, posk_ref, fwd_out, log_total, dk_acc, dv_acc,
    ssem, rsem, lsem, kvs, kvr, dsem, gsem, svsem, pairs, pairr, outsem,
):
    x, y, z, c = coords()
    cc = (x, y, z)
    bme = lax.axis_index("blk")
    eme = lax.axis_index("expert")

    def dv(dim, v, core):
        t = [x, y, z]
        t[dim] = v
        return device_of(t[0], t[1], t[2], core)

    barrier = pltpu.get_barrier_semaphore()
    peers = [dv(dim, (cc[dim] + k) & 3, c ^ dc) for dim in range(3) for k in range(1, 4) for dc in range(2)]
    peers.append(dv(0, x, c ^ 1))
    peers += [device_of(x, (y + k) & 3, z ^ 2, c) for k in range(1, 4)]
    for p in peers:
        pl.semaphore_signal(barrier, inc=1, device_id=p, device_id_type=MESH)

    pltpu.make_async_copy(down_ref, D, dsem).start()

    def gate_copy(block, slot):
        return pltpu.make_async_copy(gate_ref.at[pl.ds(block * GB, GB)], G.at[slot], gsem.at[slot])

    gate_copy(0, 0).start()
    gate_copy(1, 1).start()

    sub = lax.broadcasted_iota(jnp.int32, (128, 128), 0)
    lane = lax.broadcasted_iota(jnp.int32, (128, 128), 1)
    upper_half = jnp.where(sub < lane, 1.0, 0.0).astype(BF)
    for q in range(3):
        expert = place_expert(q, sub)
        named = jnp.zeros((128, 128), F32)
        mix = jnp.zeros((128, 128), F32)
        for k in range(8):
            match = ids_ref[k : k + 1, :] == expert
            named += jnp.where(match, 1.0, 0.0)
            mix += jnp.where(match, wts_ref[k : k + 1, :], 0.0)
        rank = jnp.dot(named.astype(BF), upper_half, preferred_element_type=F32)
        rank_ref[q] = jnp.where(named > 0.5, rank, -1.0)
        mix_ref[q] = mix

    rows = lax.broadcasted_iota(jnp.int32, (256, 256), 0)
    cols = lax.broadcasted_iota(jnp.int32, (256, 256), 1)
    perm = jnp.where(cols == (rows & 15) * 16 + (rows >> 4), 1.0, 0.0).astype(BF)

    def unpacked(lo, hi, x0):
        out = jnp.dot(perm, jnp.concatenate([lo, hi], axis=1), preferred_element_type=F32).astype(BF)
        for u in range(16):
            X[pl.ds(x0, 16), u * 128 : (u + 1) * 128] = out[u * 16 : (u + 1) * 16, :128]
            X[pl.ds(x0, 16), 2048 + u * 128 : 2048 + (u + 1) * 128] = out[u * 16 : (u + 1) * 16, 128:]

    def packed(x0):
        lo = jnp.concatenate([X[pl.ds(x0, 16), u * 128 : (u + 1) * 128] for u in range(16)], axis=0)
        hi = jnp.concatenate([X[pl.ds(x0, 16), 2048 + u * 128 : 2048 + (u + 1) * 128] for u in range(16)], axis=0)
        return jnp.dot(perm, jnp.concatenate([lo, hi], axis=1), preferred_element_type=F32).astype(BF)

    def build(j, q):
        pick = jnp.where(rank_ref[q] == float(3 * j + q), 1.0, 0.0).astype(BF)
        for h in range(4):
            X[q * 128 : (q + 1) * 128, h * 1024 : (h + 1) * 1024] = jnp.dot(
                pick, g_ref[:, h * 1024 : (h + 1) * 1024], preferred_element_type=F32
            ).astype(BF)

        def body(i, carry):
            out = packed(pl.multiple_of(q * 128 + i * 16, 16))
            at = (j * 3 + q) * 4 + i // 2
            S[at, pl.ds(i % 2 * 2, 2), :, :16, :] = out[:, :128].reshape(2, 8, 16, 128)
            S[at, pl.ds(i % 2 * 2, 2), :, 16:, :] = out[:, 128:].reshape(2, 8, 16, 128)
            return carry

        lax.fori_loop(0, 8, body, 0)

    def combine(j, halves=(0, 1)):
        if len(halves) == 2:
            def body(i, carry):
                at = j * 12 + i // 2
                lo = S[at, pl.ds(i % 2 * 2, 2), :, :16, :].reshape(256, 128)
                hi = S[at, pl.ds(i % 2 * 2, 2), :, 16:, :].reshape(256, 128)
                unpacked(lo, hi, pl.multiple_of(i * 16, 16))
                return carry

            lax.fori_loop(0, 24, body, 0)
        else:
            half = halves[0]

            def body(i, carry):
                at = j * 12 + i
                x0 = pl.multiple_of(i * 32, 32)
                lo = S[at, :2, :, half * 16 : half * 16 + 16, :].reshape(256, 128)
                hi = S[at, 2:, :, half * 16 : half * 16 + 16, :].reshape(256, 128)
                out = jnp.dot(perm, jnp.concatenate([lo, hi], axis=1), preferred_element_type=F32).astype(BF)
                for u in range(16):
                    to = slice(half * 2048 + u * 128, half * 2048 + (u + 1) * 128)
                    X[pl.ds(x0, 16), to] = out[u * 16 : (u + 1) * 16, :128]
                    X[pl.ds(x0 + 16, 16), to] = out[u * 16 : (u + 1) * 16, 128:]
                return carry

            lax.fori_loop(0, 12, body, 0)
        mix = jnp.concatenate(
            [jnp.where(rank_ref[q] == float(3 * j + q), mix_ref[q], 0.0) for q in range(3)], axis=0
        ).T.astype(BF)
        for half in halves:
            for h in (2 * half, 2 * half + 1):
                cut = slice(h * 1024, (h + 1) * 1024)
                before = g_ref[:, cut].astype(F32) if j == 0 else acc[:, cut]
                total = before + jnp.dot(mix, X[:, cut], preferred_element_type=F32)
                if j < 2:
                    acc[:, cut] = total
                else:
                    D[:128, cut] = total.astype(BF)

    def saved_copy(j):
        return pltpu.make_async_copy(saved_ref.at[pl.ds(3 * j, 3)], sv, svsem)

    saved_copy(0).start()

    for q in range(3):
        a, b, d = ORDERS[q]
        t = [None] * 3
        t[a], t[b], t[d] = sub & 3, (sub >> 2) & 3, sub >> 5
        source = t[1] * 32 + t[2] * 8 + t[0] * 2 + ((sub >> 4) & 1)
        order_ref[q] = jnp.where(lane == source, 1.0, 0.0).astype(BF)

    build(0, 0)
    pl.semaphore_wait(barrier, len(peers))

    def remote(src, dst, ph, j, q, dev):
        return pltpu.make_async_remote_copy(
            src, dst, ssem.at[ph, j, q], rsem.at[ph, j, q], device_id=dev, device_id_type=MESH
        )

    def phase(ph, j, q, half=None):
        a, b, d = ORDERS[q]
        ma, mb, md = cc[a], cc[b], cc[d]
        n = 3 * j + q
        for k in (2, 1, 3, 0):
            if ph in (0, 5):
                v = (ma + k) & 3
                if ph == 0:
                    ops = [(S.at[n * 4 + v], A.at[n, ma], dv(a, v, c), k == 0)]
                else:
                    ops = [(A.at[n, v], S.at[n * 4 + ma], dv(a, v, c), k == 0)]
            elif ph in (1, 4):
                v = (mb + k) & 3
                if ph == 1:
                    ops = [(A.at[n, :, v], B.at[n, pl.ds(mb * 4, 4)], dv(b, v, c), k == 0)]
                else:
                    ops = [(B.at[n, pl.ds(v * 4, 4)], A.at[n, :, mb], dv(b, v, c), k == 0)]
            else:
                v = (md + k) & 3
                ops = []
                for dc in range(2):
                    t = c ^ dc
                    here = k == 0 and dc == 0
                    if ph == 2:
                        ops.append((B.at[n, :, v * 2 + t], R.at[n, pl.ds((md * 2 + c) * 16, 16)], dv(d, v, t), here))
                    else:
                        ops.append((R.at[n, pl.ds((v * 2 + t) * 16, 16)], B.at[n, :, md * 2 + c], dv(d, v, t), here))
            at = j + (half or 0)
            for src, dst, dev, here in ops:
                if half is not None:
                    cut = (slice(None),) * (len(src.shape) - 2) + (pl.ds(half * 16, 16),)
                    src, dst = src.at[cut], dst.at[cut]
                if here:
                    pltpu.make_async_copy(src, dst, lsem.at[ph, at, q]).start()
                else:
                    remote(src, dst, ph, at, q, dev).start()

    def wait(ph, j, q, half=None):
        mine = 16 if ph in (2, 3) else 32
        deep = pl.ds(0, 32 if half is None else 16)
        at = j + (half or 0)
        far = R.at[0, pl.ds(0, 128 - mine), deep]
        near = R.at[0, pl.ds(0, mine), deep]
        pltpu.make_async_copy(far, far, rsem.at[ph, at, q]).wait()
        pltpu.make_async_copy(near, near, lsem.at[ph, at, q]).wait()
        pltpu.make_async_copy(far, far, ssem.at[ph, at, q]).wait()

    def experts(j):
        def unpack(i, carry):
            n = 3 * j + i // 8
            r0 = pl.multiple_of((i % 8) * 16, 16)
            lo = R[n, pl.ds(r0, 16), :16, :].reshape(256, 128)
            hi = R[n, pl.ds(r0, 16), 16:, :].reshape(256, 128)
            unpacked(lo, hi, pl.multiple_of(i * 16, 16))
            return carry

        lax.fori_loop(0, 24, unpack, 0)
        if j == 0:
            pltpu.make_async_copy(down_ref, D, dsem).wait()

        def first(i, carry):
            at = pl.multiple_of(i * 256, 256)
            dg = lax.dot_general(
                X[...], D[pl.ds(at, 256), :], (((1,), (1,)), ((), ())), preferred_element_type=F32
            )
            for q in range(3):
                cut = slice(q * 128, (q + 1) * 128)
                gate = jnp.dot(order_ref[q], sv[q, :, pl.ds(at, 256)], preferred_element_type=F32)
                upper = jnp.dot(order_ref[q], sv[q, :, pl.ds(768 + at, 256)], preferred_element_type=F32)
                sigma = 1.0 / (1.0 + jnp.exp(-gate))
                ds = dg[cut] * sigma
                act[cut, pl.ds(at, 256)] = (ds * upper * (1.0 + gate * (1.0 - sigma))).astype(BF)
                act[cut, pl.ds(768 + at, 256)] = (ds * gate).astype(BF)
            return carry

        saved_copy(j).wait()
        lax.fori_loop(0, 3, first, 0)
        if j < 2:
            saved_copy(j + 1).start()
        blocks = 4096 // GB

        def second(i, carry):
            slot = i % 2
            gate_copy(i, slot).wait()
            at = pl.multiple_of(i * GB, GB)
            X[:, pl.ds(at, GB)] = lax.dot_general(
                act[...], G[slot], (((1,), (1,)), ((), ())), preferred_element_type=F32
            ).astype(BF)
            if j < 2:
                gate_copy((i + 2) % blocks, slot).start()
            else:
                @pl.when(i < blocks - 2)
                def _():
                    gate_copy(i + 2, slot).start()
            return carry

        lax.fori_loop(0, blocks, second, 0)

        def pack(i, carry):
            n = 3 * j + i // 8
            r0 = pl.multiple_of((i % 8) * 16, 16)
            out = packed(pl.multiple_of(i * 16, 16))
            R[n, pl.ds(r0, 16), :16, :] = out[:, :128].reshape(16, 16, 128)
            R[n, pl.ds(r0, 16), 16:, :] = out[:, 128:].reshape(16, 16, 128)
            return carry

        lax.fori_loop(0, 24, pack, 0)

    def each(ph, j, half=None):
        for q in range(3):
            phase(ph, j, q, half)

    def onward(ph, j, half=None):
        for q in range(3):
            wait(ph, j, q, half)
            if ph not in (2, 5):
                phase(ph + 1, j, q, half)

    scale = 1.0 / math.sqrt(HEAD)
    nt = (((1,), (1,)), ((), ()))
    within = lax.broadcasted_iota(jnp.int32, (64, 1), 0)
    for i in range(16):
        posk_ref[i * 64 : (i + 1) * 64, :] = block_ref[i] * 64 + within
    token = lax.broadcasted_iota(jnp.int32, (1, 256), 1) & 127
    posq = jnp.where(token < 64, block_ref[2 * bme] * 64, block_ref[2 * bme + 1] * 64) + (token & 63)

    def two_heads(ref, top, h, i):
        one = pl.ds(pl.multiple_of((h * 16 + 2 * i) * 128, 128), 128)
        two = pl.ds(pl.multiple_of((h * 16 + 2 * i + 1) * 128, 128), 128)
        return jnp.concatenate([ref[top : top + 128, one], ref[top : top + 128, two]], axis=0)

    def scores_of(h, q):
        keys = kf_ref[:, :, h * 128 : (h + 1) * 128].reshape(1024, 128)
        scores = lax.dot_general(keys, q, nt, preferred_element_type=F32) * scale
        return jnp.where(posq >= posk_ref[...], scores, -1e30)

    def attention_forward(h):
        kt[h] = kf_ref[:, :, h * 128 : (h + 1) * 128].reshape(1024, 128).T
        vt[h] = vf_ref[:, :, h * 128 : (h + 1) * 128].reshape(1024, 128).T

        def tile(i, carry):
            scores = scores_of(h, two_heads(q_ref, 0, h, i))
            top = jnp.max(scores, axis=0, keepdims=True)
            weights = jnp.exp(scores - top)
            total = jnp.sum(weights, axis=0, keepdims=True)
            out = jnp.dot(vt[h], weights.astype(BF), preferred_element_type=F32) / total
            fwd_out[h * 8 + i] = out.astype(BF)
            log_total[h * 8 + i] = top + jnp.log(total)
            return carry

        lax.fori_loop(0, 8, tile, 0, unroll=2)

    def pair_copies(h):
        rows = pl.ds(256 + 128 * h, 128)
        for k in range(1, 8):
            to = (bme + k) & 7
            yield pltpu.make_async_remote_copy(
                D.at[rows, pl.ds(pl.multiple_of(to * 256, 256), 256)],
                D.at[rows, pl.ds(pl.multiple_of(2048 + bme * 256, 256), 256)],
                pairs.at[h], pairr.at[h], device_id=(to, eme), device_id_type=MESH,
            )

    def query_copy(h):
        cols = pl.ds(h * 2048, 2048)
        return pltpu.make_async_copy(D.at[pl.ds(128, 128), cols], dq_ref.at[:, cols], outsem.at[h])

    def attention_backward(h):
        dk_acc[...] = jnp.zeros_like(dk_acc)
        dv_acc[...] = jnp.zeros_like(dv_acc)

        def tile(i, carry):
            q = two_heads(q_ref, 0, h, i)
            g = two_heads(D, 0, h, i)
            delta = jnp.sum(g.astype(F32).T * fwd_out[h * 8 + i].astype(F32), axis=0, keepdims=True)
            values = vf_ref[:, :, h * 128 : (h + 1) * 128].reshape(1024, 128)
            prob_grad = lax.dot_general(values, g, nt, preferred_element_type=F32)
            probs = jnp.exp(scores_of(h, q) - log_total[h * 8 + i])
            dv_acc[...] += jnp.dot(probs.astype(BF), g, preferred_element_type=F32)
            score_grad = (probs * (prob_grad - delta)).astype(BF)
            dk_acc[...] += jnp.dot(score_grad, q, preferred_element_type=F32)
            dq = (jnp.dot(kt[h], score_grad, preferred_element_type=F32) * scale).T.astype(BF)
            D[128:256, pl.ds(pl.multiple_of((h * 16 + 2 * i) * 128, 128), 128)] = dq[:128]
            D[128:256, pl.ds(pl.multiple_of((h * 16 + 2 * i + 1) * 128, 128), 128)] = dq[128:]
            return carry

        lax.fori_loop(0, 8, tile, 0, unroll=2)
        query_copy(h).start()
        rows = slice(256 + 128 * h, 384 + 128 * h)
        for b in range(8):
            D[rows, b * 256 : b * 256 + 128] = (dk_acc[b * 128 : (b + 1) * 128, :] * scale).astype(BF)
            D[rows, b * 256 + 128 : b * 256 + 256] = dv_acc[b * 128 : (b + 1) * 128, :].astype(BF)
        for copy in pair_copies(h):
            copy.start()
        D[rows, pl.ds(pl.multiple_of(2048 + bme * 256, 256), 256)] = D[
            rows, pl.ds(pl.multiple_of(bme * 256, 256), 256)
        ]

    def pair_sums(h):
        rows = slice(256 + 128 * h, 384 + 128 * h)
        seven = D.at[pl.ds(256 + 128 * h, 128), pl.ds(0, 1792)]
        pltpu.make_async_copy(seven, seven, pairr.at[h]).wait()
        pltpu.make_async_copy(seven, seven, pairs.at[h]).wait()
        total = D[rows, 2048:2304].astype(F32)
        for b in range(1, 8):
            total += D[rows, 2048 + b * 256 : 2304 + b * 256].astype(F32)
        dk_out[:, h * 128 : (h + 1) * 128] = total[:, :128].astype(BF)
        dv_out[:, h * 128 : (h + 1) * 128] = total[:, 128:].astype(BF)

    phase(0, 0, 0)
    for q in (1, 2):
        build(0, q)
        phase(0, 0, q)
    kf_ref[bme] = k_ref[...]
    vf_ref[bme] = v_ref[...]
    for k in range(1, 8):
        to = (bme + k) & 7
        for src, dst, t in ((k_ref, kf_ref, 0), (v_ref, vf_ref, 1)):
            pltpu.make_async_remote_copy(
                src, dst.at[bme], kvs.at[t], kvr.at[t], device_id=(to, eme), device_id_type=MESH
            ).start()
    for q in range(3):
        build(1, q)
        phase(0, 1, q)
    for q in range(3):
        build(2, q)
    for t, full in ((0, kf_ref), (1, vf_ref)):
        seven = full.at[pl.ds(0, 7)]
        pltpu.make_async_copy(seven, seven, kvr.at[t]).wait()
        pltpu.make_async_copy(seven, seven, kvs.at[t]).wait()
    onward(0, 0)
    each(0, 2)
    attention_forward(0)
    onward(0, 1)
    onward(1, 0)
    attention_forward(1)
    onward(0, 2)
    onward(2, 0)
    onward(1, 1)
    experts(0)
    onward(2, 1)
    onward(1, 2)
    each(3, 0)
    experts(1)
    onward(3, 0)
    onward(2, 2)
    each(3, 1)
    experts(2)
    onward(4, 0)
    onward(3, 1)
    each(3, 2, 0)
    each(3, 2, 1)
    onward(4, 1)
    onward(3, 2, 0)
    onward(5, 0)
    combine(0)
    onward(3, 2, 1)
    onward(4, 2, 0)
    onward(5, 1)
    combine(1)
    onward(4, 2, 1)
    onward(5, 2, 0)
    combine(2, (0,))
    attention_backward(0)
    onward(5, 2, 1)
    combine(2, (1,))
    attention_backward(1)
    pair_sums(0)
    pair_sums(1)
    query_copy(0).wait()
    query_copy(1).wait()


def exchange(order, ids, wts, g, query, keys, values, saved, down, gate):
    smem = pl.BlockSpec(memory_space=pltpu.SMEM)
    vmem = pl.BlockSpec(memory_space=pltpu.VMEM)
    hbm = pl.BlockSpec(memory_space=pl.ANY)
    row = (32, 128)
    return pl.pallas_call(
        exchange_kernel,
        out_shape=(
            jax.ShapeDtypeStruct((128, 4096), BF),
            jax.ShapeDtypeStruct((128, 256), BF),
            jax.ShapeDtypeStruct((128, 256), BF),
        ),
        in_specs=[smem] + [vmem] * 6 + [hbm] * 3,
        out_specs=(hbm, vmem, vmem),
        scratch_shapes=[
            pltpu.VMEM((36, 4, 8) + row, BF),
            pltpu.VMEM((9, 4, 4, 8) + row, BF),
            pltpu.VMEM((9, 16, 8) + row, BF),
            pltpu.VMEM((9, 128) + row, BF),
            pltpu.VMEM((384, 4096), BF),
            pltpu.VMEM((384, 1536), BF),
            pltpu.VMEM((768, 4096), BF),
            pltpu.VMEM((2, GB, 1536), BF),
            pltpu.VMEM((3, 128, 1536), BF),
            pltpu.VMEM((128, 4096), F32),
            pltpu.VMEM((3, 128, 128), F32),
            pltpu.VMEM((3, 128, 128), F32),
            pltpu.VMEM((3, 128, 128), BF),
            pltpu.VMEM((8, 128, 256), BF),
            pltpu.VMEM((8, 128, 256), BF),
            pltpu.VMEM((2, 128, 1024), BF),
            pltpu.VMEM((2, 128, 1024), BF),
            pltpu.VMEM((1024, 1), jnp.int32),
            pltpu.VMEM((16, 128, 256), BF),
            pltpu.VMEM((16, 1, 256), F32),
            pltpu.VMEM((1024, 128), F32),
            pltpu.VMEM((1024, 128), F32),
            pltpu.SemaphoreType.DMA((6, 4, 3)),
            pltpu.SemaphoreType.DMA((6, 4, 3)),
            pltpu.SemaphoreType.DMA((6, 4, 3)),
            pltpu.SemaphoreType.DMA((2,)),
            pltpu.SemaphoreType.DMA((2,)),
            pltpu.SemaphoreType.DMA,
            pltpu.SemaphoreType.DMA((2,)),
            pltpu.SemaphoreType.DMA,
            pltpu.SemaphoreType.DMA((2,)),
            pltpu.SemaphoreType.DMA((2,)),
            pltpu.SemaphoreType.DMA((2,)),
        ],
        compiler_params=pltpu.CompilerParams(
            collective_id=0, has_side_effects=True, vmem_limit_bytes=63 << 20
        ),
    )(order, ids, wts, g, query, keys, values, saved, down, gate)


def handed_over_kernel(a_ref, b_ref, c_ref, a_out, b_out, c_out, sem):
    pairs = ((a_ref, a_out), (b_ref, b_out), (c_ref, c_out))
    copies = [pltpu.make_async_copy(src, dst, sem.at[i]) for i, (src, dst) in enumerate(pairs)]
    for copy in copies:
        copy.start()
    for copy in copies:
        copy.wait()


def handed_over(*arrays):
    hbm = pl.BlockSpec(memory_space=pl.ANY)
    return pl.pallas_call(
        handed_over_kernel,
        out_shape=tuple(jax.ShapeDtypeStruct(a.shape, a.dtype) for a in arrays),
        in_specs=[hbm] * 3,
        out_specs=(hbm,) * 3,
        scratch_shapes=[pltpu.SemaphoreType.DMA((3,))],
        compiler_params=pltpu.CompilerParams(vmem_limit_bytes=63 << 20),
    )(*arrays)


def local(query, keys, values, grad_output, expert_ids, gate_weights, gate_up, down_weight, saved_preact, block_order):
    dq, dk, dv = exchange(
        block_order,
        expert_ids[0].T,
        gate_weights[0].T,
        grad_output[0],
        query[0],
        keys[0],
        values[0],
        saved_preact[0].transpose(1, 0, 2),
        down_weight[0],
        gate_up[0],
    )
    dq, dk, dv = handed_over(dq, dk, dv)
    return dq[None], dk[None], dv[None]


def solution(mesh):
    token = P("expert", "blk", None)
    owner = P(("blk", "expert"), None, None)
    in_specs = (token,) * 6 + (owner, owner, P(("blk", "expert"), None, None, None), P())
    return jax.shard_map(local, mesh=mesh, in_specs=in_specs, out_specs=(token,) * 3, check_vma=False)
```

```python
import math

import jax
import jax.numpy as jnp
from jax import lax
from jax.experimental import pallas as pl
from jax.experimental.pallas import tpu as pltpu
from jax.sharding import PartitionSpec as P

MESH = pl.DeviceIdType.MESH
HEAD = 128
ORDERS = ((0, 1, 2), (1, 2, 0), (2, 0, 1))
BF = jnp.bfloat16
F32 = jnp.float32
GB = 256


def coords():
    b = lax.axis_index("blk")
    e = lax.axis_index("expert")
    return (e // 2) % 4, b // 2, (b % 2) * 2 + e // 8, e % 2


def device_of(x, y, z, c):
    return (y * 2 + z // 2, ((z % 2) * 4 + x) * 2 + c)


def place_expert(q, lane):
    a, b, d = ORDERS[q]
    t = [None] * 3
    t[a], t[b], t[d] = lane >> 5, (lane >> 3) & 3, (lane >> 1) & 3
    return t[1] * 32 + t[2] * 8 + t[0] * 2 + (lane & 1)


def exchange_kernel(
    block_ref, ids_ref, wts_ref, g_ref, q_ref, k_ref, v_ref, saved_ref, down_ref, gate_ref,
    dq_ref, dk_out, dv_out,
    S, A, B, R, X, act, D, G, sv, acc, rank_ref, mix_ref, order_ref,
    kf_ref, vf_ref, kt, vt, posk_ref, fwd_out, log_total, dk_acc, dv_acc,
    ssem, rsem, lsem, kvs, kvr, dsem, gsem, svsem, pairs, pairr, outsem,
):
    x, y, z, c = coords()
    cc = (x, y, z)
    bme = lax.axis_index("blk")
    eme = lax.axis_index("expert")

    def dv(dim, v, core):
        t = [x, y, z]
        t[dim] = v
        return device_of(t[0], t[1], t[2], core)

    barrier = pltpu.get_barrier_semaphore()
    peers = [dv(dim, (cc[dim] + k) & 3, c ^ dc) for dim in range(3) for k in range(1, 4) for dc in range(2)]
    peers.append(dv(0, x, c ^ 1))
    peers += [device_of(x, (y + k) & 3, z ^ 2, c) for k in range(1, 4)]
    for p in peers:
        pl.semaphore_signal(barrier, inc=1, device_id=p, device_id_type=MESH)

    pltpu.make_async_copy(down_ref, D, dsem).start()

    def gate_copy(block, slot):
        return pltpu.make_async_copy(gate_ref.at[pl.ds(block * GB, GB)], G.at[slot], gsem.at[slot])

    gate_copy(0, 0).start()
    gate_copy(1, 1).start()

    sub = lax.broadcasted_iota(jnp.int32, (128, 128), 0)
    lane = lax.broadcasted_iota(jnp.int32, (128, 128), 1)
    upper_half = jnp.where(sub < lane, 1.0, 0.0).astype(BF)
    for q in range(3):
        expert = place_expert(q, sub)
        named = jnp.zeros((128, 128), F32)
        mix = jnp.zeros((128, 128), F32)
        for k in range(8):
            match = ids_ref[k : k + 1, :] == expert
            named += jnp.where(match, 1.0, 0.0)
            mix += jnp.where(match, wts_ref[k : k + 1, :], 0.0)
        rank = jnp.dot(named.astype(BF), upper_half, preferred_element_type=F32)
        rank_ref[q] = jnp.where(named > 0.5, rank, -1.0)
        mix_ref[q] = mix

    rows = lax.broadcasted_iota(jnp.int32, (256, 256), 0)
    cols = lax.broadcasted_iota(jnp.int32, (256, 256), 1)
    perm = jnp.where(cols == (rows & 15) * 16 + (rows >> 4), 1.0, 0.0).astype(BF)

    def unpacked(lo, hi, x0):
        out = jnp.dot(perm, jnp.concatenate([lo, hi], axis=1), preferred_element_type=F32).astype(BF)
        for u in range(16):
            X[pl.ds(x0, 16), u * 128 : (u + 1) * 128] = out[u * 16 : (u + 1) * 16, :128]
            X[pl.ds(x0, 16), 2048 + u * 128 : 2048 + (u + 1) * 128] = out[u * 16 : (u + 1) * 16, 128:]

    def packed(x0):
        lo = jnp.concatenate([X[pl.ds(x0, 16), u * 128 : (u + 1) * 128] for u in range(16)], axis=0)
        hi = jnp.concatenate([X[pl.ds(x0, 16), 2048 + u * 128 : 2048 + (u + 1) * 128] for u in range(16)], axis=0)
        return jnp.dot(perm, jnp.concatenate([lo, hi], axis=1), preferred_element_type=F32).astype(BF)

    def build(j):
        for q in range(3):
            pick = jnp.where(rank_ref[q] == float(3 * j + q), 1.0, 0.0).astype(BF)
            for h in range(4):
                X[q * 128 : (q + 1) * 128, h * 1024 : (h + 1) * 1024] = jnp.dot(
                    pick, g_ref[:, h * 1024 : (h + 1) * 1024], preferred_element_type=F32
                ).astype(BF)

        def body(i, carry):
            out = packed(pl.multiple_of(i * 16, 16))
            at = j * 12 + i // 2
            S[at, pl.ds(i % 2 * 2, 2), :, :16, :] = out[:, :128].reshape(2, 8, 16, 128)
            S[at, pl.ds(i % 2 * 2, 2), :, 16:, :] = out[:, 128:].reshape(2, 8, 16, 128)
            return carry

        lax.fori_loop(0, 24, body, 0)

    def combine(j, halves=(0, 1)):
        if len(halves) == 2:
            def body(i, carry):
                at = j * 12 + i // 2
                lo = S[at, pl.ds(i % 2 * 2, 2), :, :16, :].reshape(256, 128)
                hi = S[at, pl.ds(i % 2 * 2, 2), :, 16:, :].reshape(256, 128)
                unpacked(lo, hi, pl.multiple_of(i * 16, 16))
                return carry

            lax.fori_loop(0, 24, body, 0)
        else:
            half = halves[0]

            def body(i, carry):
                at = j * 12 + i
                x0 = pl.multiple_of(i * 32, 32)
                lo = S[at, :2, :, half * 16 : half * 16 + 16, :].reshape(256, 128)
                hi = S[at, 2:, :, half * 16 : half * 16 + 16, :].reshape(256, 128)
                out = jnp.dot(perm, jnp.concatenate([lo, hi], axis=1), preferred_element_type=F32).astype(BF)
                for u in range(16):
                    to = slice(half * 2048 + u * 128, half * 2048 + (u + 1) * 128)
                    X[pl.ds(x0, 16), to] = out[u * 16 : (u + 1) * 16, :128]
                    X[pl.ds(x0 + 16, 16), to] = out[u * 16 : (u + 1) * 16, 128:]
                return carry

            lax.fori_loop(0, 12, body, 0)
        mix = jnp.concatenate(
            [jnp.where(rank_ref[q] == float(3 * j + q), mix_ref[q], 0.0) for q in range(3)], axis=0
        ).T.astype(BF)
        for half in halves:
            for h in (2 * half, 2 * half + 1):
                cut = slice(h * 1024, (h + 1) * 1024)
                before = g_ref[:, cut].astype(F32) if j == 0 else acc[:, cut]
                total = before + jnp.dot(mix, X[:, cut], preferred_element_type=F32)
                if j < 2:
                    acc[:, cut] = total
                else:
                    D[:128, cut] = total.astype(BF)

    def saved_copy(j):
        return pltpu.make_async_copy(saved_ref.at[pl.ds(3 * j, 3)], sv, svsem)

    saved_copy(0).start()

    for q in range(3):
        a, b, d = ORDERS[q]
        t = [None] * 3
        t[a], t[b], t[d] = sub & 3, (sub >> 2) & 3, sub >> 5
        source = t[1] * 32 + t[2] * 8 + t[0] * 2 + ((sub >> 4) & 1)
        order_ref[q] = jnp.where(lane == source, 1.0, 0.0).astype(BF)

    build(0)
    pl.semaphore_wait(barrier, len(peers))

    def remote(src, dst, ph, j, q, dev):
        return pltpu.make_async_remote_copy(
            src, dst, ssem.at[ph, j, q], rsem.at[ph, j, q], device_id=dev, device_id_type=MESH
        )

    def phase(ph, j, q, half=None):
        a, b, d = ORDERS[q]
        ma, mb, md = cc[a], cc[b], cc[d]
        n = 3 * j + q
        for k in (2, 1, 3, 0):
            if ph in (0, 5):
                v = (ma + k) & 3
                if ph == 0:
                    ops = [(S.at[n * 4 + v], A.at[n, ma], dv(a, v, c), k == 0)]
                else:
                    ops = [(A.at[n, v], S.at[n * 4 + ma], dv(a, v, c), k == 0)]
            elif ph in (1, 4):
                v = (mb + k) & 3
                if ph == 1:
                    ops = [(A.at[n, :, v], B.at[n, pl.ds(mb * 4, 4)], dv(b, v, c), k == 0)]
                else:
                    ops = [(B.at[n, pl.ds(v * 4, 4)], A.at[n, :, mb], dv(b, v, c), k == 0)]
            else:
                v = (md + k) & 3
                ops = []
                for dc in range(2):
                    t = c ^ dc
                    here = k == 0 and dc == 0
                    if ph == 2:
                        ops.append((B.at[n, :, v * 2 + t], R.at[n, pl.ds((md * 2 + c) * 16, 16)], dv(d, v, t), here))
                    else:
                        ops.append((R.at[n, pl.ds((v * 2 + t) * 16, 16)], B.at[n, :, md * 2 + c], dv(d, v, t), here))
            at = j + (half or 0)
            for src, dst, dev, here in ops:
                if half is not None:
                    cut = (slice(None),) * (len(src.shape) - 2) + (pl.ds(half * 16, 16),)
                    src, dst = src.at[cut], dst.at[cut]
                if here:
                    pltpu.make_async_copy(src, dst, lsem.at[ph, at, q]).start()
                else:
                    remote(src, dst, ph, at, q, dev).start()

    def wait(ph, j, q, half=None):
        mine = 16 if ph in (2, 3) else 32
        deep = pl.ds(0, 32 if half is None else 16)
        at = j + (half or 0)
        far = R.at[0, pl.ds(0, 128 - mine), deep]
        near = R.at[0, pl.ds(0, mine), deep]
        pltpu.make_async_copy(far, far, rsem.at[ph, at, q]).wait()
        pltpu.make_async_copy(near, near, lsem.at[ph, at, q]).wait()
        pltpu.make_async_copy(far, far, ssem.at[ph, at, q]).wait()

    def experts(j):
        def unpack(i, carry):
            n = 3 * j + i // 8
            r0 = pl.multiple_of((i % 8) * 16, 16)
            lo = R[n, pl.ds(r0, 16), :16, :].reshape(256, 128)
            hi = R[n, pl.ds(r0, 16), 16:, :].reshape(256, 128)
            unpacked(lo, hi, pl.multiple_of(i * 16, 16))
            return carry

        lax.fori_loop(0, 24, unpack, 0)
        if j == 0:
            pltpu.make_async_copy(down_ref, D, dsem).wait()

        def first(i, carry):
            at = pl.multiple_of(i * 256, 256)
            dg = lax.dot_general(
                X[...], D[pl.ds(at, 256), :], (((1,), (1,)), ((), ())), preferred_element_type=F32
            )
            for q in range(3):
                cut = slice(q * 128, (q + 1) * 128)
                gate = jnp.dot(order_ref[q], sv[q, :, pl.ds(at, 256)], preferred_element_type=F32)
                upper = jnp.dot(order_ref[q], sv[q, :, pl.ds(768 + at, 256)], preferred_element_type=F32)
                sigma = 1.0 / (1.0 + jnp.exp(-gate))
                ds = dg[cut] * sigma
                act[cut, pl.ds(at, 256)] = (ds * upper * (1.0 + gate * (1.0 - sigma))).astype(BF)
                act[cut, pl.ds(768 + at, 256)] = (ds * gate).astype(BF)
            return carry

        saved_copy(j).wait()
        lax.fori_loop(0, 3, first, 0)
        if j < 2:
            saved_copy(j + 1).start()
        blocks = 4096 // GB

        def second(i, carry):
            slot = i % 2
            gate_copy(i, slot).wait()
            at = pl.multiple_of(i * GB, GB)
            X[:, pl.ds(at, GB)] = lax.dot_general(
                act[...], G[slot], (((1,), (1,)), ((), ())), preferred_element_type=F32
            ).astype(BF)
            if j < 2:
                gate_copy((i + 2) % blocks, slot).start()
            else:
                @pl.when(i < blocks - 2)
                def _():
                    gate_copy(i + 2, slot).start()
            return carry

        lax.fori_loop(0, blocks, second, 0)

        def pack(i, carry):
            n = 3 * j + i // 8
            r0 = pl.multiple_of((i % 8) * 16, 16)
            out = packed(pl.multiple_of(i * 16, 16))
            R[n, pl.ds(r0, 16), :16, :] = out[:, :128].reshape(16, 16, 128)
            R[n, pl.ds(r0, 16), 16:, :] = out[:, 128:].reshape(16, 16, 128)
            return carry

        lax.fori_loop(0, 24, pack, 0)

    def each(ph, j, half=None):
        for q in range(3):
            phase(ph, j, q, half)

    def onward(ph, j, half=None):
        for q in range(3):
            wait(ph, j, q, half)
            if ph not in (2, 5):
                phase(ph + 1, j, q, half)

    scale = 1.0 / math.sqrt(HEAD)
    nt = (((1,), (1,)), ((), ()))
    within = lax.broadcasted_iota(jnp.int32, (64, 1), 0)
    for i in range(16):
        posk_ref[i * 64 : (i + 1) * 64, :] = block_ref[i] * 64 + within
    token = lax.broadcasted_iota(jnp.int32, (1, 256), 1) & 127
    posq = jnp.where(token < 64, block_ref[2 * bme] * 64, block_ref[2 * bme + 1] * 64) + (token & 63)

    def two_heads(ref, top, h, i):
        one = pl.ds(pl.multiple_of((h * 16 + 2 * i) * 128, 128), 128)
        two = pl.ds(pl.multiple_of((h * 16 + 2 * i + 1) * 128, 128), 128)
        return jnp.concatenate([ref[top : top + 128, one], ref[top : top + 128, two]], axis=0)

    def scores_of(h, q):
        keys = kf_ref[:, :, h * 128 : (h + 1) * 128].reshape(1024, 128)
        scores = lax.dot_general(keys, q, nt, preferred_element_type=F32) * scale
        return jnp.where(posq >= posk_ref[...], scores, -1e30)

    def attention_forward(h):
        kt[h] = kf_ref[:, :, h * 128 : (h + 1) * 128].reshape(1024, 128).T
        vt[h] = vf_ref[:, :, h * 128 : (h + 1) * 128].reshape(1024, 128).T

        def tile(i, carry):
            scores = scores_of(h, two_heads(q_ref, 0, h, i))
            top = jnp.max(scores, axis=0, keepdims=True)
            weights = jnp.exp(scores - top)
            total = jnp.sum(weights, axis=0, keepdims=True)
            out = jnp.dot(vt[h], weights.astype(BF), preferred_element_type=F32) / total
            fwd_out[h * 8 + i] = out.astype(BF)
            log_total[h * 8 + i] = top + jnp.log(total)
            return carry

        lax.fori_loop(0, 8, tile, 0)

    def pair_copies(h):
        rows = pl.ds(256 + 128 * h, 128)
        for k in range(1, 8):
            to = (bme + k) & 7
            yield pltpu.make_async_remote_copy(
                D.at[rows, pl.ds(pl.multiple_of(to * 256, 256), 256)],
                D.at[rows, pl.ds(pl.multiple_of(2048 + bme * 256, 256), 256)],
                pairs.at[h], pairr.at[h], device_id=(to, eme), device_id_type=MESH,
            )

    def query_copy(h):
        cols = pl.ds(h * 2048, 2048)
        return pltpu.make_async_copy(D.at[pl.ds(128, 128), cols], dq_ref.at[:, cols], outsem.at[h])

    def attention_backward(h):
        dk_acc[...] = jnp.zeros_like(dk_acc)
        dv_acc[...] = jnp.zeros_like(dv_acc)

        def tile(i, carry):
            q = two_heads(q_ref, 0, h, i)
            g = two_heads(D, 0, h, i)
            delta = jnp.sum(g.astype(F32).T * fwd_out[h * 8 + i].astype(F32), axis=0, keepdims=True)
            values = vf_ref[:, :, h * 128 : (h + 1) * 128].reshape(1024, 128)
            prob_grad = lax.dot_general(values, g, nt, preferred_element_type=F32)
            probs = jnp.exp(scores_of(h, q) - log_total[h * 8 + i])
            dv_acc[...] += jnp.dot(probs.astype(BF), g, preferred_element_type=F32)
            score_grad = (probs * (prob_grad - delta)).astype(BF)
            dk_acc[...] += jnp.dot(score_grad, q, preferred_element_type=F32)
            dq = (jnp.dot(kt[h], score_grad, preferred_element_type=F32) * scale).T.astype(BF)
            D[128:256, pl.ds(pl.multiple_of((h * 16 + 2 * i) * 128, 128), 128)] = dq[:128]
            D[128:256, pl.ds(pl.multiple_of((h * 16 + 2 * i + 1) * 128, 128), 128)] = dq[128:]
            return carry

        lax.fori_loop(0, 8, tile, 0)
        query_copy(h).start()
        rows = slice(256 + 128 * h, 384 + 128 * h)
        for b in range(8):
            D[rows, b * 256 : b * 256 + 128] = (dk_acc[b * 128 : (b + 1) * 128, :] * scale).astype(BF)
            D[rows, b * 256 + 128 : b * 256 + 256] = dv_acc[b * 128 : (b + 1) * 128, :].astype(BF)
        for copy in pair_copies(h):
            copy.start()
        D[rows, pl.ds(pl.multiple_of(2048 + bme * 256, 256), 256)] = D[
            rows, pl.ds(pl.multiple_of(bme * 256, 256), 256)
        ]

    def pair_sums(h):
        rows = slice(256 + 128 * h, 384 + 128 * h)
        seven = D.at[pl.ds(256 + 128 * h, 128), pl.ds(0, 1792)]
        pltpu.make_async_copy(seven, seven, pairr.at[h]).wait()
        pltpu.make_async_copy(seven, seven, pairs.at[h]).wait()
        total = D[rows, 2048:2304].astype(F32)
        for b in range(1, 8):
            total += D[rows, 2048 + b * 256 : 2304 + b * 256].astype(F32)
        dk_out[:, h * 128 : (h + 1) * 128] = total[:, :128].astype(BF)
        dv_out[:, h * 128 : (h + 1) * 128] = total[:, 128:].astype(BF)

    each(0, 0)
    kf_ref[bme] = k_ref[...]
    vf_ref[bme] = v_ref[...]
    for k in range(1, 8):
        to = (bme + k) & 7
        for src, dst, t in ((k_ref, kf_ref, 0), (v_ref, vf_ref, 1)):
            pltpu.make_async_remote_copy(
                src, dst.at[bme], kvs.at[t], kvr.at[t], device_id=(to, eme), device_id_type=MESH
            ).start()
    build(1)
    onward(0, 0)
    each(0, 1)
    build(2)
    for t, full in ((0, kf_ref), (1, vf_ref)):
        seven = full.at[pl.ds(0, 7)]
        pltpu.make_async_copy(seven, seven, kvr.at[t]).wait()
        pltpu.make_async_copy(seven, seven, kvs.at[t]).wait()
    attention_forward(0)
    onward(1, 0)
    onward(0, 1)
    each(0, 2)
    attention_forward(1)
    onward(2, 0)
    onward(1, 1)
    onward(0, 2)
    experts(0)
    onward(2, 1)
    onward(1, 2)
    each(3, 0)
    experts(1)
    onward(3, 0)
    onward(2, 2)
    each(3, 1)
    experts(2)
    onward(4, 0)
    onward(3, 1)
    each(3, 2, 0)
    each(3, 2, 1)
    onward(5, 0)
    combine(0)
    onward(4, 1)
    onward(3, 2, 0)
    onward(3, 2, 1)
    onward(5, 1)
    combine(1)
    onward(4, 2, 0)
    onward(4, 2, 1)
    onward(5, 2, 0)
    combine(2, (0,))
    attention_backward(0)
    onward(5, 2, 1)
    combine(2, (1,))
    attention_backward(1)
    pair_sums(0)
    pair_sums(1)
    query_copy(0).wait()
    query_copy(1).wait()


def exchange(order, ids, wts, g, query, keys, values, saved, down, gate):
    smem = pl.BlockSpec(memory_space=pltpu.SMEM)
    vmem = pl.BlockSpec(memory_space=pltpu.VMEM)
    hbm = pl.BlockSpec(memory_space=pl.ANY)
    row = (32, 128)
    return pl.pallas_call(
        exchange_kernel,
        out_shape=(
            jax.ShapeDtypeStruct((128, 4096), BF),
            jax.ShapeDtypeStruct((128, 256), BF),
            jax.ShapeDtypeStruct((128, 256), BF),
        ),
        in_specs=[smem] + [vmem] * 6 + [hbm] * 3,
        out_specs=(hbm, vmem, vmem),
        scratch_shapes=[
            pltpu.VMEM((36, 4, 8) + row, BF),
            pltpu.VMEM((9, 4, 4, 8) + row, BF),
            pltpu.VMEM((9, 16, 8) + row, BF),
            pltpu.VMEM((9, 128) + row, BF),
            pltpu.VMEM((384, 4096), BF),
            pltpu.VMEM((384, 1536), BF),
            pltpu.VMEM((768, 4096), BF),
            pltpu.VMEM((2, GB, 1536), BF),
            pltpu.VMEM((3, 128, 1536), BF),
            pltpu.VMEM((128, 4096), F32),
            pltpu.VMEM((3, 128, 128), F32),
            pltpu.VMEM((3, 128, 128), F32),
            pltpu.VMEM((3, 128, 128), BF),
            pltpu.VMEM((8, 128, 256), BF),
            pltpu.VMEM((8, 128, 256), BF),
            pltpu.VMEM((2, 128, 1024), BF),
            pltpu.VMEM((2, 128, 1024), BF),
            pltpu.VMEM((1024, 1), jnp.int32),
            pltpu.VMEM((16, 128, 256), BF),
            pltpu.VMEM((16, 1, 256), F32),
            pltpu.VMEM((1024, 128), F32),
            pltpu.VMEM((1024, 128), F32),
            pltpu.SemaphoreType.DMA((6, 4, 3)),
            pltpu.SemaphoreType.DMA((6, 4, 3)),
            pltpu.SemaphoreType.DMA((6, 4, 3)),
            pltpu.SemaphoreType.DMA((2,)),
            pltpu.SemaphoreType.DMA((2,)),
            pltpu.SemaphoreType.DMA,
            pltpu.SemaphoreType.DMA((2,)),
            pltpu.SemaphoreType.DMA,
            pltpu.SemaphoreType.DMA((2,)),
            pltpu.SemaphoreType.DMA((2,)),
            pltpu.SemaphoreType.DMA((2,)),
        ],
        compiler_params=pltpu.CompilerParams(
            collective_id=0, has_side_effects=True, vmem_limit_bytes=63 << 20
        ),
    )(order, ids, wts, g, query, keys, values, saved, down, gate)


def handed_over_kernel(a_ref, b_ref, c_ref, a_out, b_out, c_out):
    a_out[...] = a_ref[...]
    b_out[...] = b_ref[...]
    c_out[...] = c_ref[...]


def handed_over(*arrays):
    specs = [pl.BlockSpec((64, a.shape[1]), lambda i: (i, 0)) for a in arrays]
    return pl.pallas_call(
        handed_over_kernel,
        grid=(2,),
        out_shape=tuple(jax.ShapeDtypeStruct(a.shape, a.dtype) for a in arrays),
        in_specs=specs,
        out_specs=specs,
        compiler_params=pltpu.CompilerParams(vmem_limit_bytes=63 << 20),
    )(*arrays)


def local(query, keys, values, grad_output, expert_ids, gate_weights, gate_up, down_weight, saved_preact, block_order):
    dq, dk, dv = exchange(
        block_order,
        expert_ids[0].T,
        gate_weights[0].T,
        grad_output[0],
        query[0],
        keys[0],
        values[0],
        saved_preact[0].transpose(1, 0, 2),
        down_weight[0],
        gate_up[0],
    )
    dq, dk, dv = handed_over(dq, dk, dv)
    return dq[None], dk[None], dv[None]


def solution(mesh):
    token = P("expert", "blk", None)
    owner = P(("blk", "expert"), None, None)
    in_specs = (token,) * 6 + (owner, owner, P(("blk", "expert"), None, None, None), P())
    return jax.shard_map(local, mesh=mesh, in_specs=in_specs, out_specs=(token,) * 3, check_vma=False)
```
